32 devices in a mesh: tm: 8 (over z, x), rows: 4 (over y, core).
Axes of the slice: x: 2, y: 2, z: 4, core: 2. Of those that a mesh axis runs over, the one named last changes fastest.
Arguments:
- x_start: float32 [1, 16, 64, 128], P(None, None, 'rows'), may hold values from -6 to 6
- noise: float32 [8, 1, 16, 64, 128], P('tm', None, None, 'rows'), may hold values from -6 to 6
- fresh: float32 [5, 1, 16, 64, 128], P(None, None, None, 'rows'), may hold values from -6 to 6
- sched: int32 [14], replicated, may hold values from 960 to 999, as said below
- conv_in: bfloat16 [3, 3, 192, 16], replicated, may hold values from -0.5 to 0.5
- conv_mid: bfloat16 [3, 3, 192, 192], replicated, may hold values from -0.15625 to 0.15625
- conv_out: bfloat16 [3, 3, 16, 192], replicated, may hold values from -0.15625 to 0.15625
- time_weight: bfloat16 [192, 192], replicated, may hold values from -0.4375 to 0.4375
Outputs:
- trajectory: float32 [2, 8, 1, 16, 64, 128], P(None, 'tm', None, None, 'rows')
The draws below stay inside these ranges and needn't reach their ends.
Inputs may be any that keep to these rules, and one draw needn't show every extreme that they name: sched[0] = 999 and each entry is 1 to 3 below the one before it.
All inputs are finite; a program needn't handle non-finite values.
Results may differ from the reference program's by a relative error of at most 0.00055.
Values may be sent and summed in bfloat16 or wider, within the bound.
A program may use at most 64 MiB of HBM per device.

```python
import jax
import jax.numpy as jnp
from jax import lax

LAT_CH = 16
HIDDEN_SIZE = 192
COLS = 128
FRAMES = 1
STEPS = 1000
SWEEPS = 2
RETIRE = 5
ROUNDS = 2
WINDOW = 8
HEIGHT = 64
SPAN = 14


def draw_sched(key, part):
    strides = jax.random.randint(key, (SPAN,), 1, 4)
    strides = jnp.where(jnp.arange(SPAN) == 0, 0, strides)
    return (STEPS - 1 - jnp.cumsum(strides)).astype(jnp.int32)


def shard_levels(key, shape, pieces, least, top_value):
    def one(axis_at, parts):
        heights = jax.random.uniform(jax.random.fold_in(jax.random.fold_in(key, 6), axis_at), (parts,), jnp.float32, least / len(pieces), top_value / len(pieces))
        return jnp.repeat(jnp.exp(heights), shape[axis_at] // parts).reshape((-1,) + (1,) * (len(shape) - axis_at - 1))

    gain = one(*pieces[0])
    for cut in pieces[1:]:
        gain = gain * one(*cut)
    return gain


def centred(stream_key, extent, deviation, most, split=(), kind=jnp.bfloat16):
    array = deviation * jax.random.normal(stream_key, extent, jnp.float32)
    if split:
        array = array * shard_levels(stream_key, extent, split, -0.22, 0.18)
    return jnp.clip(array, -most, most).astype(kind)


def setup_inputs(seed: int = 0) -> dict:
    arg_keys = jax.random.split(jax.random.key(seed), 9)
    x_start = centred(arg_keys[0], (FRAMES, LAT_CH, HEIGHT, COLS), 1.0, 6.0, ((2, 4),), jnp.float32)
    noise = centred(arg_keys[1], (WINDOW, FRAMES, LAT_CH, HEIGHT, COLS), 1.0, 6.0, ((0, 8), (3, 4)), jnp.float32)
    fresh = centred(arg_keys[2], ((ROUNDS - 1) * RETIRE, FRAMES, LAT_CH, HEIGHT, COLS), 1.0, 6.0, ((3, 4),), jnp.float32)
    sched = draw_sched(jax.random.fold_in(arg_keys[8], 71), 0)
    conv_in = centred(arg_keys[4], (3, 3, HIDDEN_SIZE, LAT_CH), (9 * LAT_CH) ** -0.5, 0.5)
    conv_mid = centred(arg_keys[5], (3, 3, HIDDEN_SIZE, HIDDEN_SIZE), (9 * HIDDEN_SIZE) ** -0.5, 0.15625)
    conv_out = centred(arg_keys[6], (3, 3, LAT_CH, HIDDEN_SIZE), (9 * HIDDEN_SIZE) ** -0.5, 0.15625)
    time_weight = centred(arg_keys[7], (HIDDEN_SIZE, HIDDEN_SIZE), HIDDEN_SIZE ** -0.5, 0.4375)
    return {"x_start": x_start, "noise": noise, "fresh": fresh, "sched": sched, "conv_in": conv_in, "conv_mid": conv_mid, "conv_out": conv_out, "time_weight": time_weight}


log_base = 9.210340371976184

def plan_table(total_steps):
    positions = jnp.arange(total_steps).astype(jnp.float32)
    betas = 0.0001 + (0.02 - 0.0001) * positions / (total_steps - 1)
    return jnp.cumsum(jnp.log(1.0 - betas))

def coefficients(log_now, log_next):
    retained = jnp.exp(log_now - log_next)
    bar_now = jnp.exp(log_now)
    bar_next = jnp.exp(log_next)
    keep = 1.0 / jnp.sqrt(retained) - 1.0
    predict = -(1.0 - retained) / (jnp.sqrt(1.0 - bar_now) * jnp.sqrt(retained))
    spread = jnp.sqrt((1.0 - bar_next) / (1.0 - bar_now) * (1.0 - retained))
    return (keep, predict, spread)

def time_features(now_value, width):
    half = width // 2
    freqs = jnp.exp(-log_base * jnp.arange(half).astype(jnp.float32) / half)
    angles = now_value[..., None] * freqs
    return jnp.concatenate([jnp.sin(angles), jnp.cos(angles)], axis=-1)

def convolve_full(values, weight):
    widened = jnp.pad(values, ((0, 0), (0, 0), (0, 0), (1, 1), (1, 1)))
    height, columns = (values.shape[3], values.shape[4])
    running = jnp.zeros(values.shape[:2] + (weight.shape[2], height, columns), jnp.float32)
    for row_tap in range(3):
        for col_tap in range(3):
            shifted = widened[:, :, :, row_tap:row_tap + height, col_tap:col_tap + columns]
            running = running + jnp.einsum('oc,sfcrw->sforw', weight[row_tap, col_tap].astype(jnp.float32), shifted, precision=lax.Precision.HIGHEST)
    return running

def rounded(values):
    return lax.optimization_barrier(values.astype(jnp.bfloat16)).astype(jnp.float32)

def network(state, embedding, conv_in, conv_mid, conv_out):
    latent = rounded(state)
    first = convolve_full(latent, conv_in) + embedding[:, None, :, None, None]
    first = rounded(jax.nn.silu(first))
    second = rounded(jax.nn.silu(convolve_full(first, conv_mid)))
    return convolve_full(second, conv_out)

def reference(x_start, noise, fresh, sched, conv_in, conv_mid, conv_out, time_weight):
    table = plan_table(STEPS)
    state = jnp.broadcast_to(x_start[None], (WINDOW,) + x_start.shape)
    noise_now = noise
    base_state = x_start
    snapshots = []
    for round_index in range(ROUNDS):
        offset = RETIRE * round_index
        now_steps = sched[offset:offset + WINDOW]
        next_steps = sched[offset + 1:offset + WINDOW + 1]
        keep, predict, spread = coefficients(table[now_steps], table[next_steps])
        features = time_features(now_steps.astype(jnp.float32), HIDDEN_SIZE)
        embedding = jnp.dot(features, time_weight.astype(jnp.float32), precision=lax.Precision.HIGHEST)
        for sweep_index in range(SWEEPS):
            predicted = network(state, embedding, conv_in, conv_mid, conv_out)
            change = keep[:, None, None, None, None] * state + predict[:, None, None, None, None] * predicted + spread[:, None, None, None, None] * noise_now
            running = jnp.cumsum(change, axis=0)
            prior = jnp.concatenate([jnp.zeros_like(change[:1]), running[:-1]], axis=0)
            state = base_state[None] + prior
        snapshots.append(state)
        if round_index + 1 < ROUNDS:
            state = jnp.concatenate([state[RETIRE:], state[WINDOW - RETIRE:]], axis=0)
            noise_now = jnp.concatenate([noise_now[RETIRE:], fresh[round_index * RETIRE:(round_index + 1) * RETIRE]], axis=0)
            base_state = state[0]
    return jnp.stack(snapshots)
```

```python
import functools

import jax
import jax.numpy as jnp
import numpy as np
from jax import lax
from jax.experimental import pallas as pl
from jax.experimental.pallas import tpu as pltpu
from jax.sharding import PartitionSpec as P

STEPS = 1000
RETIRE = 5
ROUNDS = 2
RIM = 3

log_base = 9.210340371976184
MESH = pl.DeviceIdType.MESH
f32, bf16 = jnp.float32, jnp.bfloat16


def plan_table(total_steps):
    positions = np.arange(total_steps).astype(np.float64)
    betas = 0.0001 + (0.02 - 0.0001) * positions / (total_steps - 1)
    return jnp.asarray(np.cumsum(np.log(1.0 - betas)).astype(np.float32))


def lookup(table, position):
    hit = jnp.arange(table.shape[0])[None] == position[:, None]
    return jnp.sum(jnp.where(hit, table[None], 0.0), axis=1)


def coefficients(log_now, log_next):
    retained = jnp.exp(log_now - log_next)
    bar_now = jnp.exp(log_now)
    bar_next = jnp.exp(log_next)
    keep = 1.0 / jnp.sqrt(retained) - 1.0
    predict = -(1.0 - retained) / (jnp.sqrt(1.0 - bar_now) * jnp.sqrt(retained))
    spread = jnp.sqrt((1.0 - bar_next) / (1.0 - bar_now) * (1.0 - retained))
    return jnp.stack([keep, predict, spread], axis=1)


def time_features(now_value, width):
    half = width // 2
    freqs = jnp.exp(-log_base * jnp.arange(half).astype(f32) / half)
    angles = now_value[..., None] * freqs
    return jnp.concatenate([jnp.sin(angles), jnp.cos(angles)], axis=-1)


def silu(v):
    half = 0.5 * v
    return half + half * jnp.tanh(half)


def moved_right(v):
    lane = lax.broadcasted_iota(jnp.int32, v.shape, v.ndim - 1)
    return jnp.where(lane == 0, 0.0, pltpu.roll(v, 1, v.ndim - 1))


def moved_left(v):
    size = v.shape[-1]
    lane = lax.broadcasted_iota(jnp.int32, v.shape, v.ndim - 1)
    return jnp.where(lane == size - 1, 0.0, pltpu.roll(v, size - 1, v.ndim - 1))


def kernel(
    n, strips, hops,
    coef, x, z0, entrant, emb, w_in, w_mid, w_out, out,
    st, first, parts, state, exc, inc, nexc, ninc, base, base_src,
    sent_state, rim, arrived, z_arrived,
    snd, rcv, nsnd, nrcv,
    rim_ss, rim_rs, far_ss, mv_ss, mv_rs, z_ss, z_rs,
    scan_ss, scan_rs, nscan_ss, nscan_rs, base_ss, base_rs,
):
    me, strip = lax.axis_index("tm"), lax.axis_index("rows")
    rows, chans, cols = x.shape
    hidden = w_mid.shape[0]
    stay = n - RETIRE
    has_up, has_down = strip > 0, strip < strips - 1

    def remote(src, dst, ss, rs, slot, to_strip):
        return pltpu.make_async_remote_copy(
            src_ref=src, dst_ref=dst, send_sem=ss, recv_sem=rs,
            device_id=(jnp.clip(slot, 0, n - 1), jnp.clip(to_strip, 0, strips - 1)),
            device_id_type=MESH,
        )

    def rim_copy(k, side, slot, far):
        lo = rows - RIM if side == 0 else 0
        to = strip + 1 if side == 0 else strip - 1
        ss = far_ss.at[side] if far else rim_ss.at[k, side]
        return remote(sent_state.at[k, pl.ds(lo, RIM)], rim.at[k, side], ss, rim_rs.at[k, side], slot, to)

    def send_rim(k, slot, far, gate, start):
        for side, there in ((0, has_down), (1, has_up)):
            @pl.when(jnp.logical_and(gate, there))
            def _():
                copy = rim_copy(k, side, slot, far)
                copy.start() if start else copy.wait_send()

    def move_copy():
        return remote(sent_state.at[2], arrived, mv_ss, mv_rs, me - RETIRE, strip)

    def z_copy():
        return remote(z0, z_arrived, z_ss, z_rs, me - RETIRE, strip)

    def base_copy(slot):
        return remote(base_src, base, base_ss.at[slot], base_rs, slot, strip)

    def scan_copy(k, s):
        return remote(snd.at[k, s], rcv.at[k, s], scan_ss.at[k, s], scan_rs.at[k, s], me + 2**s, strip)

    def nscan_copy(k, s):
        return remote(nsnd.at[k, s], nrcv.at[k, s], nscan_ss.at[k, s], nscan_rs.at[k, s], me + 2**s, strip)

    def spread_rows(v):
        v = v.astype(f32)
        return jnp.concatenate([moved_right(v), v, moved_left(v)], axis=-2).astype(bf16)

    def expand(source, at, count):
        for i in range(count):
            st[at + i] = spread_rows(source[i])

    def noise_send(k, s):
        @pl.when(me + 2**s < n)
        def _():
            nsnd[k, s] = ninc[k]
            nscan_copy(k, s).start()

    def noise_take(k, s):
        @pl.when(me >= 2**s)
        def _():
            nscan_copy(k, s).wait_recv()
            nexc[k] += nrcv[k, s]
            ninc[k] += nrcv[k, s]

    def noise_advance(k, s):
        if s < hops:
            noise_take(k, s)
        if s + 1 < hops:
            noise_send(k, s + 1)

    def noise_finish(k, s):
        for t in range(s, hops):
            noise_advance(k, t)

    def network(r):
        embedding = emb.at[r]

        def in_step(i, _):
            f = 2 * i
            both = jnp.concatenate(
                [st[pl.ds(f + t, 3)].reshape(9 * chans, cols) for t in range(2)], axis=1
            )
            h = jnp.dot(w_in[...], both, preferred_element_type=f32)
            for t in range(2):
                v = silu(h[:, t * cols : (t + 1) * cols] + embedding[...])
                first[f + t] = spread_rows(v)
            return 0

        lax.fori_loop(0, (rows + 4) // 2, in_step, 0, unroll=2)

        @pl.when(jnp.logical_not(has_up))
        def _():
            first[pl.ds(0, 2)] = jnp.zeros((2,) + first.shape[1:], bf16)

        @pl.when(jnp.logical_not(has_down))
        def _():
            first[pl.ds(rows + 2, 2)] = jnp.zeros((2,) + first.shape[1:], bf16)

        def mid_step(i, _):
            f = 2 * i
            both = jnp.concatenate(
                [first[pl.ds(f + t, 3)].reshape(9 * hidden, cols) for t in range(2)], axis=1
            )
            g = silu(jnp.dot(w_mid[...], both, preferred_element_type=f32)).astype(bf16)
            p = jnp.dot(w_out[...], g, preferred_element_type=f32)
            for t in range(2):
                parts[f + t] = p[:, t * cols : (t + 1) * cols]
            return 0

        lax.fori_loop(0, (rows + 2) // 2, mid_step, 0, unroll=3)

        @pl.when(jnp.logical_not(has_up))
        def _():
            parts[0] = jnp.zeros(parts.shape[1:], f32)

        @pl.when(jnp.logical_not(has_down))
        def _():
            parts[rows + 1] = jnp.zeros(parts.shape[1:], f32)

    def finish(k, r, noise):
        keep, predict, spread = coef[r, 0], coef[r, 1], coef[r, 2]

        def row(y, _):
            sums = [
                sum(parts[y + a, pl.ds((3 * a + b) * chans, chans)] for a in range(3))
                for b in range(3)
            ]
            predicted = moved_right(sums[0]) + sums[1] + moved_left(sums[2])
            c = keep * state[y] + predict * predicted
            if noise is not None:
                c = c + spread * noise[y]
            inc[y] = c
            exc[y] = jnp.zeros_like(c)
            snd[k, 0, y] = c.astype(bf16)
            return 0

        lax.fori_loop(0, rows, row, 0, unroll=4)

    def scan(k):
        for s in range(hops):
            @pl.when(me + 2**s < n)
            def _():
                if s > 0:
                    snd[k, s] = inc[...].astype(bf16)
                scan_copy(k, s).start()

            @pl.when(me >= 2**s)
            def _():
                scan_copy(k, s).wait_recv()
                got = rcv[k, s].astype(f32)
                exc[...] += got
                if s + 1 < hops:
                    inc[...] += got

    def take_rim(k):
        for side, there in ((0, has_up), (1, has_down)):
            @pl.when(there)
            def _():
                rim_copy(k, side, me, False).wait_recv()
                expand(rim.at[k, side], 0 if side == 0 else rows + RIM, RIM)

    yes = me >= 0

    sent_state[0] = x[...].astype(bf16)
    send_rim(0, me, False, yes, True)

    @pl.when(me >= RETIRE)
    def _():
        z_copy().start()

    nexc[...] = jnp.zeros(nexc.shape, f32)
    ninc[0] = coef[0, 2] * z0[...]
    noise_send(0, 0)
    state[...] = x[...]

    @pl.when(jnp.logical_not(has_up))
    def _():
        st[pl.ds(0, RIM)] = jnp.zeros((RIM,) + st.shape[1:], bf16)

    @pl.when(jnp.logical_not(has_down))
    def _():
        st[pl.ds(rows + RIM, RIM)] = jnp.zeros((RIM,) + st.shape[1:], bf16)

    expand(x, RIM, rows)
    take_rim(0)
    network(0)
    finish(0, 0, z0)
    noise_advance(0, 0)
    scan(0)
    state[...] = x[...] + exc[...]
    sent_state[1] = state[...].astype(bf16)
    send_rim(1, me, False, yes, True)
    expand(state, RIM, rows)
    noise_advance(0, 1)

    @pl.when(me < stay)
    def _():
        z_copy().wait_recv()

    @pl.when(me >= stay)
    def _():
        z_arrived[...] = entrant[...]

    ninc[1] = coef[1, 2] * z_arrived[...]
    noise_send(1, 0)

    take_rim(1)
    network(0)
    finish(1, 0, None)
    scan(1)
    noise_finish(0, 2)
    state[...] = x[...] + (nexc[0] + exc[...])
    out[0] = state[...]

    sent_state[2] = state[...].astype(bf16)

    @pl.when(me >= RETIRE)
    def _():
        move_copy().start()

    send_rim(2, me - RETIRE, True, me >= RETIRE, True)
    send_rim(2, me, False, me >= stay, True)
    base_src[...] = state[...]

    @pl.when(me == RETIRE)
    def _():
        base[...] = base_src[...]
        for slot in range(n):
            if slot != RETIRE:
                base_copy(slot).start()

    noise_advance(1, 0)

    @pl.when(me < stay)
    def _():
        move_copy().wait_recv()
        state[...] = arrived[...].astype(f32)

    expand(state, RIM, rows)
    take_rim(2)
    network(1)
    finish(2, 1, z_arrived)
    scan(2)

    @pl.when(me != RETIRE)
    def _():
        base_copy(0).wait_recv()

    state[...] = base[...] + exc[...]
    sent_state[3] = state[...].astype(bf16)
    send_rim(3, me, False, yes, True)
    expand(state, RIM, rows)
    noise_advance(1, 1)
    take_rim(3)
    network(1)
    finish(3, 1, None)
    scan(3)
    noise_finish(1, 2)
    out[1] = base[...] + (nexc[1] + exc[...])

    for k, gate in ((0, yes), (1, yes), (2, me >= stay), (3, yes)):
        send_rim(k, me, False, gate, False)
    send_rim(2, me - RETIRE, True, me >= RETIRE, False)

    @pl.when(me >= RETIRE)
    def _():
        z_copy().wait_send()
        move_copy().wait_send()

    @pl.when(me == RETIRE)
    def _():
        for slot in range(n):
            if slot != RETIRE:
                base_copy(slot).wait_send()

    for s in range(hops):
        @pl.when(me + 2**s < n)
        def _():
            for k in range(4):
                scan_copy(k, s).wait_send()
            for k in range(2):
                nscan_copy(k, s).wait_send()


def shards(x_start, noise, fresh, sched, conv_in, conv_mid, conv_out, time_weight):
    slot, n, strips = lax.axis_index("tm"), lax.axis_size("tm"), lax.axis_size("rows")
    hidden, chans, rows, cols = conv_mid.shape[2], x_start.shape[1], x_start.shape[2], x_start.shape[3]
    hops = (n - 1).bit_length()
    table = plan_table(STEPS)
    spots = [lax.dynamic_slice_in_dim(sched, slot + RETIRE * r, 2, 0) for r in range(ROUNDS)]
    steps = jnp.stack(spots)
    logs = lookup(table, steps.reshape(-1)).reshape(ROUNDS, 2)
    coef = coefficients(logs[:, 0], logs[:, 1])
    features = time_features(steps[:, 0].astype(f32), hidden)
    embedding = jnp.dot(features, time_weight.astype(f32), precision=lax.Precision.HIGHEST)
    emb = jnp.broadcast_to(embedding[:, :, None], (ROUNDS, hidden, cols))
    pick = jnp.clip(slot - (n - RETIRE), 0, fresh.shape[0] - 1)
    entrant = lax.dynamic_index_in_dim(fresh, pick, 0, keepdims=False)[0].transpose(1, 0, 2)
    x = x_start[0].transpose(1, 0, 2)
    z = noise[0, 0].transpose(1, 0, 2)
    w_in = conv_in.transpose(2, 0, 1, 3).reshape(hidden, -1)
    w_mid = conv_mid.transpose(2, 0, 1, 3).reshape(hidden, -1)
    w_out = conv_out.reshape(-1, hidden)

    frame = (rows, chans, cols)
    vmem, dma = pltpu.VMEM, pltpu.SemaphoreType.DMA
    result = pl.pallas_call(
        functools.partial(kernel, n, strips, hops),
        out_shape=jax.ShapeDtypeStruct((ROUNDS,) + frame, f32),
        in_specs=[pl.BlockSpec(memory_space=pltpu.SMEM)] + [pl.BlockSpec(memory_space=pltpu.VMEM)] * 7,
        out_specs=pl.BlockSpec(memory_space=pltpu.VMEM),
        scratch_shapes=[
            vmem((rows + 2 * RIM, 3 * chans, cols), bf16),
            vmem((rows + 4, 3 * hidden, cols), bf16),
            vmem((rows + 2, 9 * chans, cols), f32),
            vmem(frame, f32),
            vmem(frame, f32),
            vmem(frame, f32),
            vmem((2,) + frame, f32),
            vmem((2,) + frame, f32),
            vmem(frame, f32),
            vmem(frame, f32),
            vmem((4,) + frame, bf16),
            vmem((4, 2, RIM, chans, cols), bf16),
            vmem(frame, bf16),
            vmem(frame, f32),
            vmem((4, hops) + frame, bf16),
            vmem((4, hops) + frame, bf16),
            vmem((2, hops) + frame, f32),
            vmem((2, hops) + frame, f32),
            dma((4, 2)),
            dma((4, 2)),
            dma((2,)),
            dma,
            dma,
            dma,
            dma,
            dma((4, hops)),
            dma((4, hops)),
            dma((2, hops)),
            dma((2, hops)),
            dma((n,)),
            dma,
        ],
        compiler_params=pltpu.CompilerParams(has_side_effects=True, vmem_limit_bytes=48 * 2**20),
        cost_estimate=pl.CostEstimate(
            flops=8 * rows * cols * 9 * hidden * (hidden + 2 * chans),
            bytes_accessed=4 * 2**20,
            transcendentals=8 * rows * cols * hidden,
        ),
    )(coef, x, z, entrant, emb, w_in, w_mid, w_out)
    return result.transpose(0, 2, 1, 3)[:, None, None]


def solution(mesh):
    placed = (
        P(None, None, "rows", None),
        P("tm", None, None, "rows", None),
        P(None, None, None, "rows", None),
        P(),
        P(),
        P(),
        P(),
        P(),
    )
    return jax.shard_map(
        shards,
        mesh=mesh,
        in_specs=placed,
        out_specs=P(None, "tm", None, None, "rows", None),
        check_vma=False,
    )
```

```python
import functools

import jax
import jax.numpy as jnp
import numpy as np
from jax import lax
from jax.experimental import pallas as pl
from jax.experimental.pallas import tpu as pltpu
from jax.sharding import PartitionSpec as P

STEPS = 1000
RETIRE = 5
ROUNDS = 2
RIM = 3

log_base = 9.210340371976184
MESH = pl.DeviceIdType.MESH
f32, bf16 = jnp.float32, jnp.bfloat16


def plan_table(total_steps):
    positions = np.arange(total_steps).astype(np.float64)
    betas = 0.0001 + (0.02 - 0.0001) * positions / (total_steps - 1)
    return jnp.asarray(np.cumsum(np.log(1.0 - betas)).astype(np.float32))


def lookup(table, position):
    hit = jnp.arange(table.shape[0])[None] == position[:, None]
    return jnp.sum(jnp.where(hit, table[None], 0.0), axis=1)


def coefficients(log_now, log_next):
    retained = jnp.exp(log_now - log_next)
    bar_now = jnp.exp(log_now)
    bar_next = jnp.exp(log_next)
    keep = 1.0 / jnp.sqrt(retained) - 1.0
    predict = -(1.0 - retained) / (jnp.sqrt(1.0 - bar_now) * jnp.sqrt(retained))
    spread = jnp.sqrt((1.0 - bar_next) / (1.0 - bar_now) * (1.0 - retained))
    return jnp.stack([keep, predict, spread], axis=1)


def time_features(now_value, width):
    half = width // 2
    freqs = jnp.exp(-log_base * jnp.arange(half).astype(f32) / half)
    angles = now_value[..., None] * freqs
    return jnp.concatenate([jnp.sin(angles), jnp.cos(angles)], axis=-1)


def silu(v):
    half = 0.5 * v
    return half + half * jnp.tanh(half)


def moved_right(v):
    lane = lax.broadcasted_iota(jnp.int32, v.shape, v.ndim - 1)
    return jnp.where(lane == 0, 0.0, pltpu.roll(v, 1, v.ndim - 1))


def moved_left(v):
    size = v.shape[-1]
    lane = lax.broadcasted_iota(jnp.int32, v.shape, v.ndim - 1)
    return jnp.where(lane == size - 1, 0.0, pltpu.roll(v, size - 1, v.ndim - 1))


def kernel(
    n, strips, hops,
    coef, x_far, z_far, fresh_far, emb_far, in_far, mid_far, out_far, out,
    x_raw, z_raw, fresh_raw, emb, in_raw, mid_raw, w_out, x, z0, w_in, w_mid,
    st, first, parts, state, exc, inc, nexc, ninc, base, base_src,
    sent_state, rim, arrived, z_arrived,
    snd, rcv, nsnd, nrcv,
    rim_ss, rim_rs, far_ss, mv_ss, mv_rs, z_ss, z_rs,
    scan_ss, scan_rs, nscan_ss, nscan_rs, base_ss, base_rs, load_s,
):
    me, strip = lax.axis_index("tm"), lax.axis_index("rows")
    rows, chans, cols = x.shape
    hidden = w_mid.shape[0]
    half = rows // 2
    stay = n - RETIRE
    pick = jnp.clip(me - stay, 0, fresh_far.shape[0] - 1)
    loads = [
        pltpu.make_async_copy(source, target, load_s.at[i])
        for i, (source, target) in enumerate((
            (x_far.at[0], x_raw), (in_far, in_raw), (emb_far, emb), (mid_far, mid_raw),
            (out_far, w_out), (z_far.at[0, 0], z_raw), (fresh_far.at[pick, 0], fresh_raw),
        ))
    ]
    for load in loads:
        load.start()
    has_up, has_down = strip > 0, strip < strips - 1

    def remote(src, dst, ss, rs, slot, to_strip):
        return pltpu.make_async_remote_copy(
            src_ref=src, dst_ref=dst, send_sem=ss, recv_sem=rs,
            device_id=(jnp.clip(slot, 0, n - 1), jnp.clip(to_strip, 0, strips - 1)),
            device_id_type=MESH,
        )

    def rim_copy(k, side, slot, far):
        lo = rows - RIM if side == 0 else 0
        to = strip + 1 if side == 0 else strip - 1
        ss = far_ss.at[side] if far else rim_ss.at[k, side]
        return remote(sent_state.at[k, pl.ds(lo, RIM)], rim.at[k, side], ss, rim_rs.at[k, side], slot, to)

    def send_rim(k, slot, far, gate, start):
        for side, there in ((0, has_down), (1, has_up)):
            @pl.when(jnp.logical_and(gate, there))
            def _():
                copy = rim_copy(k, side, slot, far)
                copy.start() if start else copy.wait_send()

    def move_copy():
        return remote(sent_state.at[2], arrived, mv_ss, mv_rs, me - RETIRE, strip)

    def z_copy():
        return remote(z0, z_arrived, z_ss, z_rs, me - RETIRE, strip)

    def base_copy(slot):
        return remote(base_src, base, base_ss.at[slot], base_rs, slot, strip)

    def scan_copy(k, s, part):
        at = pl.ds(part * half, half)
        return remote(
            snd.at[k, s, at], rcv.at[k, s, at], scan_ss.at[k, s, part], scan_rs.at[k, s, part], me + 2**s, strip
        )

    def scan_send(k, s, part):
        if s >= hops:
            return

        @pl.when(me + 2**s < n)
        def _():
            at = pl.ds(part * half, half)
            if s > 0:
                snd[k, s, at] = inc[at].astype(bf16)
            scan_copy(k, s, part).start()

    def scan_take(k, s, part):
        if s >= hops:
            return

        @pl.when(me >= 2**s)
        def _():
            at = pl.ds(part * half, half)
            scan_copy(k, s, part).wait_recv()
            got = rcv[k, s, at].astype(f32)
            exc[at] += got
            if s + 1 < hops:
                inc[at] += got

    def nscan_copy(k, s):
        return remote(nsnd.at[k, s], nrcv.at[k, s], nscan_ss.at[k, s], nscan_rs.at[k, s], me + 2**s, strip)

    def spread_rows(v):
        v = v.astype(f32)
        return jnp.concatenate([moved_right(v), v, moved_left(v)], axis=-2).astype(bf16)

    def expand(source, at, count):
        for i in range(count):
            st[at + i] = spread_rows(source[i])

    def noise_send(k, s):
        @pl.when(me + 2**s < n)
        def _():
            nsnd[k, s] = ninc[k]
            nscan_copy(k, s).start()

    def noise_take(k, s):
        @pl.when(me >= 2**s)
        def _():
            nscan_copy(k, s).wait_recv()
            nexc[k] += nrcv[k, s]
            ninc[k] += nrcv[k, s]

    def noise_advance(k, s):
        if s < hops:
            noise_take(k, s)
        if s + 1 < hops:
            noise_send(k, s + 1)

    def noise_finish(k, s):
        for t in range(s, hops):
            noise_advance(k, t)

    def sweep(k, r, noise):
        keep, predict, spread = coef[r, 0], coef[r, 1], coef[r, 2]
        up_scale, down_scale = has_up.astype(f32), has_down.astype(f32)
        in_steps, mid_steps = (rows + 4) // 2, (rows + 2) // 2

        def in_step(i):
            f = 2 * i
            both = jnp.concatenate(
                [st[f + t : f + t + 3].reshape(9 * chans, cols) for t in range(2)], axis=1
            )
            h = jnp.dot(w_in[...], both, preferred_element_type=f32)
            for t in range(2):
                v = silu(h[:, t * cols : (t + 1) * cols] + emb[r])
                if i == 0:
                    v = v * up_scale
                if i == in_steps - 1:
                    v = v * down_scale
                first[f + t] = spread_rows(v)

        def mid_step(i):
            f = 2 * i
            both = jnp.concatenate(
                [first[f + t : f + t + 3].reshape(9 * hidden, cols) for t in range(2)], axis=1
            )
            g = silu(jnp.dot(w_mid[...], both, preferred_element_type=f32)).astype(bf16)
            p = jnp.dot(w_out[...], g, preferred_element_type=f32)
            for t in range(2):
                v = p[:, t * cols : (t + 1) * cols]
                if f + t == 0:
                    v = v * up_scale
                if f + t == rows + 1:
                    v = v * down_scale
                parts[f + t] = v

        def finish(y):
            sums = [
                sum(parts[y + a, (3 * a + b) * chans : (3 * a + b + 1) * chans] for a in range(3))
                for b in range(3)
            ]
            predicted = moved_right(sums[0]) + sums[1] + moved_left(sums[2])
            c = keep * state[y] + predict * predicted
            if noise is not None:
                c = c + spread * noise[y]
            inc[y] = c
            exc[y] = jnp.zeros_like(c)
            snd[k, 0, y] = c.astype(bf16)

        in_step(0)
        in_step(1)
        sent_at = half // 2
        for i in range(mid_steps):
            if i + 2 < in_steps:
                in_step(i + 2)
            mid_step(i)
            if i > 0:
                finish(2 * i - 2)
                finish(2 * i - 1)
            if i == sent_at:
                scan_send(k, 0, 0)
            if i == sent_at + 2:
                scan_take(k, 0, 0)
                scan_send(k, 1, 0)
        scan_send(k, 0, 1)
        for s in range(hops):
            if s > 0:
                scan_take(k, s, 0)
                scan_send(k, s + 1, 0)
            scan_take(k, s, 1)
            scan_send(k, s + 1, 1)

    def take_rim(k):
        for side, there in ((0, has_up), (1, has_down)):
            @pl.when(there)
            def _():
                rim_copy(k, side, me, False).wait_recv()
                expand(rim.at[k, side], 0 if side == 0 else rows + RIM, RIM)

    yes = me >= 0

    loads[0].wait()
    x[...] = jnp.swapaxes(x_raw[...], 0, 1)
    sent_state[0] = x[...].astype(bf16)
    send_rim(0, me, False, yes, True)
    loads[5].wait()
    z0[...] = jnp.swapaxes(z_raw[...], 0, 1)

    @pl.when(me >= RETIRE)
    def _():
        z_copy().start()

    nexc[...] = jnp.zeros(nexc.shape, f32)
    ninc[0] = coef[0, 2] * z0[...]
    noise_send(0, 0)
    state[...] = x[...]

    @pl.when(jnp.logical_not(has_up))
    def _():
        st[pl.ds(0, RIM)] = jnp.zeros((RIM,) + st.shape[1:], bf16)

    @pl.when(jnp.logical_not(has_down))
    def _():
        st[pl.ds(rows + RIM, RIM)] = jnp.zeros((RIM,) + st.shape[1:], bf16)

    expand(x, RIM, rows)
    for i in (1, 2, 3, 4, 6):
        loads[i].wait()
    taps = [(a, b) for a in range(3) for b in range(3)]
    w_in[...] = in_raw[...].astype(f32).T.astype(bf16)
    w_mid[...] = jnp.concatenate([mid_raw[a, b] for a, b in taps], axis=1)
    take_rim(0)
    sweep(0, 0, z0)
    noise_advance(0, 0)
    state[...] = x[...] + exc[...]
    sent_state[1] = state[...].astype(bf16)
    send_rim(1, me, False, yes, True)
    expand(state, RIM, rows)
    noise_advance(0, 1)

    @pl.when(me < stay)
    def _():
        z_copy().wait_recv()

    @pl.when(me >= stay)
    def _():
        z_arrived[...] = jnp.swapaxes(fresh_raw[...], 0, 1)

    ninc[1] = coef[1, 2] * z_arrived[...]
    noise_send(1, 0)

    take_rim(1)
    sweep(1, 0, None)
    noise_finish(0, 2)
    state[...] = x[...] + (nexc[0] + exc[...])
    out[0] = state[...]

    sent_state[2] = state[...].astype(bf16)

    @pl.when(me >= RETIRE)
    def _():
        move_copy().start()

    send_rim(2, me - RETIRE, True, me >= RETIRE, True)
    send_rim(2, me, False, me >= stay, True)
    base_src[...] = state[...]

    @pl.when(me == RETIRE)
    def _():
        base[...] = base_src[...]
        for slot in range(n):
            if slot != RETIRE:
                base_copy(slot).start()

    noise_advance(1, 0)

    @pl.when(me < stay)
    def _():
        move_copy().wait_recv()
        state[...] = arrived[...].astype(f32)

    expand(state, RIM, rows)
    take_rim(2)
    sweep(2, 1, z_arrived)

    @pl.when(me != RETIRE)
    def _():
        base_copy(0).wait_recv()

    state[...] = base[...] + exc[...]
    sent_state[3] = state[...].astype(bf16)
    send_rim(3, me, False, yes, True)
    expand(state, RIM, rows)
    noise_advance(1, 1)
    take_rim(3)
    sweep(3, 1, None)
    noise_finish(1, 2)
    out[1] = base[...] + (nexc[1] + exc[...])

    for k, gate in ((0, yes), (1, yes), (2, me >= stay), (3, yes)):
        send_rim(k, me, False, gate, False)
    send_rim(2, me - RETIRE, True, me >= RETIRE, False)

    @pl.when(me >= RETIRE)
    def _():
        z_copy().wait_send()
        move_copy().wait_send()

    @pl.when(me == RETIRE)
    def _():
        for slot in range(n):
            if slot != RETIRE:
                base_copy(slot).wait_send()

    for s in range(hops):
        @pl.when(me + 2**s < n)
        def _():
            for k in range(4):
                scan_copy(k, s, 0).wait_send()
                scan_copy(k, s, 1).wait_send()
            for k in range(2):
                nscan_copy(k, s).wait_send()


def shards(x_start, noise, fresh, sched, conv_in, conv_mid, conv_out, time_weight):
    slot, n, strips = lax.axis_index("tm"), lax.axis_size("tm"), lax.axis_size("rows")
    hidden, chans, rows, cols = conv_mid.shape[2], x_start.shape[1], x_start.shape[2], x_start.shape[3]
    hops = (n - 1).bit_length()
    table = plan_table(STEPS)
    spots = [lax.dynamic_slice_in_dim(sched, slot + RETIRE * r, 2, 0) for r in range(ROUNDS)]
    steps = jnp.stack(spots)
    logs = lookup(table, steps.reshape(-1)).reshape(ROUNDS, 2)
    coef = coefficients(logs[:, 0], logs[:, 1])
    features = time_features(steps[:, 0].astype(f32), hidden)
    embedding = jnp.dot(features, time_weight.astype(f32), precision=lax.Precision.HIGHEST)
    emb = jnp.broadcast_to(embedding[:, :, None], (ROUNDS, hidden, cols))
    frame = (rows, chans, cols)
    vmem, dma = pltpu.VMEM, pltpu.SemaphoreType.DMA
    result = pl.pallas_call(
        functools.partial(kernel, n, strips, hops),
        out_shape=jax.ShapeDtypeStruct((ROUNDS,) + frame, f32),
        in_specs=[pl.BlockSpec(memory_space=pltpu.SMEM)] + [pl.BlockSpec(memory_space=pltpu.HBM)] * 7,
        out_specs=pl.BlockSpec(memory_space=pltpu.VMEM),
        scratch_shapes=[
            vmem((chans, rows, cols), f32),
            vmem((chans, rows, cols), f32),
            vmem((chans, rows, cols), f32),
            vmem((ROUNDS, hidden, cols), f32),
            vmem((9 * chans, hidden), bf16),
            vmem(conv_mid.shape, bf16),
            vmem((9 * chans, hidden), bf16),
            vmem(frame, f32),
            vmem(frame, f32),
            vmem((hidden, 9 * chans), bf16),
            vmem((hidden, 9 * hidden), bf16),
            vmem((rows + 2 * RIM, 3 * chans, cols), bf16),
            vmem((rows + 4, 3 * hidden, cols), bf16),
            vmem((rows + 2, 9 * chans, cols), f32),
            vmem(frame, f32),
            vmem(frame, f32),
            vmem(frame, f32),
            vmem((2,) + frame, f32),
            vmem((2,) + frame, f32),
            vmem(frame, f32),
            vmem(frame, f32),
            vmem((4,) + frame, bf16),
            vmem((4, 2, RIM, chans, cols), bf16),
            vmem(frame, bf16),
            vmem(frame, f32),
            vmem((4, hops) + frame, bf16),
            vmem((4, hops) + frame, bf16),
            vmem((2, hops) + frame, f32),
            vmem((2, hops) + frame, f32),
            dma((4, 2)),
            dma((4, 2)),
            dma((2,)),
            dma,
            dma,
            dma,
            dma,
            dma((4, hops, 2)),
            dma((4, hops, 2)),
            dma((2, hops)),
            dma((2, hops)),
            dma((n,)),
            dma,
            dma((7,)),
        ],
        compiler_params=pltpu.CompilerParams(has_side_effects=True, vmem_limit_bytes=56 * 2**20),
        cost_estimate=pl.CostEstimate(
            flops=8 * rows * cols * 9 * hidden * (hidden + 2 * chans),
            bytes_accessed=4 * 2**20,
            transcendentals=8 * rows * cols * hidden,
        ),
    )(coef, x_start, noise, fresh, emb, conv_in.transpose(0, 1, 3, 2).reshape(-1, hidden), conv_mid, conv_out.reshape(-1, hidden))
    return result.transpose(0, 2, 1, 3)[:, None, None]


def solution(mesh):
    placed = (
        P(None, None, "rows", None),
        P("tm", None, None, "rows", None),
        P(None, None, None, "rows", None),
        P(),
        P(),
        P(),
        P(),
        P(),
    )
    return jax.shard_map(
        shards,
        mesh=mesh,
        in_specs=placed,
        out_specs=P(None, "tm", None, None, "rows", None),
        check_vma=False,
    )
```

```python
import functools

import jax
import jax.numpy as jnp
import numpy as np
from jax import lax
from jax.experimental import pallas as pl
from jax.experimental.pallas import tpu as pltpu
from jax.sharding import PartitionSpec as P

STEPS = 1000
RETIRE = 5
ROUNDS = 2
RIM = 3

log_base = 9.210340371976184
MESH = pl.DeviceIdType.MESH
f32, bf16 = jnp.float32, jnp.bfloat16


def plan_table(total_steps):
    positions = np.arange(total_steps).astype(np.float64)
    betas = 0.0001 + (0.02 - 0.0001) * positions / (total_steps - 1)
    return jnp.asarray(np.cumsum(np.log(1.0 - betas)).astype(np.float32))


def lookup(table, position):
    hit = jnp.arange(table.shape[0])[None] == position[:, None]
    return jnp.sum(jnp.where(hit, table[None], 0.0), axis=1)


def coefficients(log_now, log_next):
    retained = jnp.exp(log_now - log_next)
    bar_now = jnp.exp(log_now)
    bar_next = jnp.exp(log_next)
    keep = 1.0 / jnp.sqrt(retained) - 1.0
    predict = -(1.0 - retained) / (jnp.sqrt(1.0 - bar_now) * jnp.sqrt(retained))
    spread = jnp.sqrt((1.0 - bar_next) / (1.0 - bar_now) * (1.0 - retained))
    return jnp.stack([keep, predict, spread], axis=1)


def time_features(now_value, width):
    half = width // 2
    freqs = jnp.exp(-log_base * jnp.arange(half).astype(f32) / half)
    angles = now_value[..., None] * freqs
    return jnp.concatenate([jnp.sin(angles), jnp.cos(angles)], axis=-1)


def silu(v):
    half = 0.5 * v
    return half + half * jnp.tanh(half)


def moved_right(v):
    lane = lax.broadcasted_iota(jnp.int32, v.shape, v.ndim - 1)
    return jnp.where(lane == 0, 0.0, pltpu.roll(v, 1, v.ndim - 1))


def moved_left(v):
    size = v.shape[-1]
    lane = lax.broadcasted_iota(jnp.int32, v.shape, v.ndim - 1)
    return jnp.where(lane == size - 1, 0.0, pltpu.roll(v, size - 1, v.ndim - 1))


def kernel(
    n, strips, hops,
    coef, x_far, z_far, fresh_far, emb, in_far, mid_far, out_far, out,
    x_raw, z_raw, fresh_raw, in_raw, mid_raw, w_out, x, z0, w_in, w_mid,
    st, first, parts, state, exc, inc, nexc, ninc, base,
    sent_state, rim, arrived, z_arrived,
    snd, rcv, nsnd, nrcv,
    rim_ss, rim_rs, far_ss, mv_ss, mv_rs, z_ss, z_rs,
    scan_ss, scan_rs, nscan_ss, nscan_rs, base_ss, base_rs, load_s,
):
    me, strip = lax.axis_index("tm"), lax.axis_index("rows")
    rows, chans, cols = x.shape
    hidden = w_mid.shape[0]
    half = rows // 2
    stay = n - RETIRE
    pick = jnp.clip(me - stay, 0, fresh_far.shape[0] - 1)
    loads = [
        pltpu.make_async_copy(source, target, load_s.at[i])
        for i, (source, target) in enumerate((
            (x_far.at[0], x_raw), (in_far, in_raw), (mid_far, mid_raw),
            (out_far, w_out), (z_far.at[0, 0], z_raw), (fresh_far.at[pick, 0], fresh_raw),
        ))
    ]
    for load in loads:
        load.start()
    has_up, has_down = strip > 0, strip < strips - 1

    def remote(src, dst, ss, rs, slot, to_strip):
        return pltpu.make_async_remote_copy(
            src_ref=src, dst_ref=dst, send_sem=ss, recv_sem=rs,
            device_id=(jnp.clip(slot, 0, n - 1), jnp.clip(to_strip, 0, strips - 1)),
            device_id_type=MESH,
        )

    def rim_copy(k, side, slot, far):
        lo = rows - RIM if side == 0 else 0
        to = strip + 1 if side == 0 else strip - 1
        ss = far_ss.at[side] if far else rim_ss.at[k, side]
        return remote(sent_state.at[k, pl.ds(lo, RIM)], rim.at[k, side], ss, rim_rs.at[k, side], slot, to)

    def send_rim(k, slot, far, gate, start):
        for side, there in ((0, has_down), (1, has_up)):
            @pl.when(jnp.logical_and(gate, there))
            def _():
                copy = rim_copy(k, side, slot, far)
                copy.start() if start else copy.wait_send()

    def move_copy():
        return remote(sent_state.at[2], arrived, mv_ss, mv_rs, me - RETIRE, strip)

    def z_copy():
        return remote(z0, z_arrived, z_ss, z_rs, me - RETIRE, strip)

    def base_copy(to, lane):
        return remote(base, base, base_ss.at[lane], base_rs, to, strip)

    mate = RETIRE + 1 - 2 * (RETIRE % 2)
    low, high = min(RETIRE, mate), max(RETIRE, mate)
    base_moves = (
        (me == RETIRE, mate, 0),
        (jnp.logical_and(me <= high, me >= 2), me - 2, 1),
        (jnp.logical_and(me >= low, me + 2 < n), me + 2, 2),
    )

    def base_pass(gate):
        @pl.when(jnp.logical_and(gate, me != RETIRE))
        def _():
            base_copy(me, 0).wait_recv()

        for allowed, to, lane in base_moves:
            @pl.when(jnp.logical_and(gate, allowed))
            def _():
                base_copy(to, lane).start()

    def scan_copy(k, s, part):
        at = pl.ds(part * half, half)
        return remote(
            snd.at[k, s, at], rcv.at[k, s, at], scan_ss.at[k, s, part], scan_rs.at[k, s, part], me + 2**s, strip
        )

    def scan_send(k, s, part):
        if s >= hops:
            return

        @pl.when(me + 2**s < n)
        def _():
            at = pl.ds(part * half, half)
            if s > 0:
                snd[k, s, at] = inc[at].astype(bf16)
            scan_copy(k, s, part).start()

    def scan_take(k, s, part):
        if s >= hops:
            return

        @pl.when(me >= 2**s)
        def _():
            at = pl.ds(part * half, half)
            scan_copy(k, s, part).wait_recv()
            got = rcv[k, s, at].astype(f32)
            exc[at] += got
            if s + 1 < hops:
                inc[at] += got

    level, odd = me // 2, me % 2

    def nscan_copy(k, s):
        to = me + 1 - 2 * odd if s == 0 else me + 2
        return remote(nsnd.at[k, s], nrcv.at[k, s], nscan_ss.at[k, s], nscan_rs.at[k, s], to, strip)

    def spread_rows(v):
        v = v.astype(f32)
        return jnp.concatenate([moved_right(v), v, moved_left(v)], axis=-2).astype(bf16)

    def expand(source, at, count):
        for i in range(count):
            st[at + i] = spread_rows(source[i])

    def noise_start(k, z):
        nsnd[k, 0] = coef[k, 2] * z[...]
        nscan_copy(k, 0).start()

    def noise_pair(k):
        nscan_copy(k, 0).wait_recv()
        ninc[k] = nsnd[k, 0] + nrcv[k, 0]
        nexc[k] = nrcv[k, 0] * odd.astype(f32)

    def noise_pass(k, gate):
        @pl.when(jnp.logical_and(gate, level > 0))
        def _():
            nscan_copy(k, 1).wait_recv()
            nexc[k] += nrcv[k, 1]
            ninc[k] += nrcv[k, 1]

        @pl.when(jnp.logical_and(gate, me + 2 < n))
        def _():
            nsnd[k, 1] = ninc[k]
            nscan_copy(k, 1).start()

    def sweep(k, r, noise, hooks=()):
        keep, predict, spread = coef[r, 0], coef[r, 1], coef[r, 2]
        up_scale, down_scale = has_up.astype(f32), has_down.astype(f32)
        in_steps, mid_steps = (rows + 4) // 2, (rows + 2) // 2

        def in_step(i):
            f = 2 * i
            both = jnp.concatenate(
                [st[f + t : f + t + 3].reshape(9 * chans, cols) for t in range(2)], axis=1
            )
            h = jnp.dot(w_in[...], both, preferred_element_type=f32)
            for t in range(2):
                v = silu(h[:, t * cols : (t + 1) * cols] + emb[r])
                if i == 0:
                    v = v * up_scale
                if i == in_steps - 1:
                    v = v * down_scale
                first[f + t] = spread_rows(v)

        def mid_step(i):
            f = 2 * i
            both = jnp.concatenate(
                [first[f + t : f + t + 3].reshape(9 * hidden, cols) for t in range(2)], axis=1
            )
            g = silu(jnp.dot(w_mid[...], both, preferred_element_type=f32)).astype(bf16)
            p = jnp.dot(w_out[...], g, preferred_element_type=f32)
            for t in range(2):
                v = p[:, t * cols : (t + 1) * cols]
                if f + t == 0:
                    v = v * up_scale
                if f + t == rows + 1:
                    v = v * down_scale
                parts[f + t] = v

        def finish(y):
            sums = [
                sum(parts[y + a, (3 * a + b) * chans : (3 * a + b + 1) * chans] for a in range(3))
                for b in range(3)
            ]
            predicted = moved_right(sums[0]) + sums[1] + moved_left(sums[2])
            c = keep * state[y] + predict * predicted
            if noise is not None:
                c = c + spread * noise[y]
            inc[y] = c
            exc[y] = jnp.zeros_like(c)
            snd[k, 0, y] = c.astype(bf16)

        in_step(0)
        in_step(1)
        sent_at = half // 2
        for i in range(mid_steps):
            if i + 2 < in_steps:
                in_step(i + 2)
            mid_step(i)
            if i > 0:
                finish(2 * i - 2)
                finish(2 * i - 1)
            if i == sent_at:
                scan_send(k, 0, 0)
            for at, hook in hooks:
                if i == at:
                    hook()
            if i == sent_at + 2:
                scan_take(k, 0, 0)
                scan_send(k, 1, 0)
        scan_send(k, 0, 1)
        for s in range(hops):
            if s > 0:
                scan_take(k, s, 0)
                scan_send(k, s + 1, 0)
            scan_take(k, s, 1)
            scan_send(k, s + 1, 1)

    def take_rim(k):
        for side, there in ((0, has_up), (1, has_down)):
            @pl.when(there)
            def _():
                rim_copy(k, side, me, False).wait_recv()
                expand(rim.at[k, side], 0 if side == 0 else rows + RIM, RIM)

    yes = me >= 0
    early, late = 2, rows // 2 - 1

    loads[0].wait()
    x[...] = jnp.swapaxes(x_raw[...], 0, 1)
    sent_state[0] = x[...].astype(bf16)
    send_rim(0, me, False, yes, True)
    loads[4].wait()
    z0[...] = jnp.swapaxes(z_raw[...], 0, 1)

    @pl.when(me >= RETIRE)
    def _():
        z_copy().start()

    noise_start(0, z0)
    state[...] = x[...]

    @pl.when(jnp.logical_not(has_up))
    def _():
        st[pl.ds(0, RIM)] = jnp.zeros((RIM,) + st.shape[1:], bf16)

    @pl.when(jnp.logical_not(has_down))
    def _():
        st[pl.ds(rows + RIM, RIM)] = jnp.zeros((RIM,) + st.shape[1:], bf16)

    expand(x, RIM, rows)
    for i in (1, 2, 3, 5):
        loads[i].wait()
    taps = [(a, b) for a in range(3) for b in range(3)]
    w_in[...] = in_raw[...].astype(f32).T.astype(bf16)
    w_mid[...] = jnp.concatenate([mid_raw[a, b] for a, b in taps], axis=1)
    take_rim(0)
    def first_pairs():
        noise_pair(0)
        noise_pass(0, level == 0)

    sweep(0, 0, z0, ((early, first_pairs),))
    state[...] = x[...] + exc[...]
    sent_state[1] = state[...].astype(bf16)
    send_rim(1, me, False, yes, True)
    expand(state, RIM, rows)
    noise_pass(0, level == 1)

    @pl.when(me < stay)
    def _():
        z_copy().wait_recv()

    @pl.when(me >= stay)
    def _():
        z_arrived[...] = jnp.swapaxes(fresh_raw[...], 0, 1)

    noise_start(1, z_arrived)

    take_rim(1)
    def second_pairs():
        noise_pass(0, level == 2)
        noise_pair(1)
        noise_pass(1, level == 0)

    sweep(1, 0, None, ((early, second_pairs),))
    noise_pass(0, level >= 3)
    state[...] = x[...] + (nexc[0] + exc[...])
    out[0] = state[...]

    sent_state[2] = state[...].astype(bf16)

    @pl.when(me >= RETIRE)
    def _():
        move_copy().start()

    send_rim(2, me - RETIRE, True, me >= RETIRE, True)
    send_rim(2, me, False, me >= stay, True)

    @pl.when(me == RETIRE)
    def _():
        base[...] = state[...]

    base_pass(me == RETIRE)
    noise_pass(1, level == 1)

    @pl.when(me < stay)
    def _():
        move_copy().wait_recv()
        state[...] = arrived[...].astype(f32)

    expand(state, RIM, rows)
    take_rim(2)
    near = jnp.logical_or(me == mate, me == RETIRE - 2)
    next_near = me == mate - 2

    def base_far():
        base_pass(next_near)
        noise_pass(1, level == 2)

    sweep(2, 1, z_arrived, ((early, lambda: base_pass(near)), (late, base_far)))

    base_pass(jnp.logical_not(jnp.logical_or(me == RETIRE, jnp.logical_or(near, next_near))))
    state[...] = base[...] + exc[...]
    sent_state[3] = state[...].astype(bf16)
    send_rim(3, me, False, yes, True)
    expand(state, RIM, rows)
    take_rim(3)
    sweep(3, 1, None)
    noise_pass(1, level >= 3)
    out[1] = base[...] + (nexc[1] + exc[...])

    for k, gate in ((0, yes), (1, yes), (2, me >= stay), (3, yes)):
        send_rim(k, me, False, gate, False)
    send_rim(2, me - RETIRE, True, me >= RETIRE, False)

    @pl.when(me >= RETIRE)
    def _():
        z_copy().wait_send()
        move_copy().wait_send()

    for allowed, to, lane in base_moves:
        @pl.when(allowed)
        def _():
            base_copy(to, lane).wait_send()

    for k in range(2):
        nscan_copy(k, 0).wait_send()

        @pl.when(me + 2 < n)
        def _():
            nscan_copy(k, 1).wait_send()

    for s in range(hops):
        @pl.when(me + 2**s < n)
        def _():
            for k in range(4):
                scan_copy(k, s, 0).wait_send()
                scan_copy(k, s, 1).wait_send()


def shards(x_start, noise, fresh, sched, conv_in, conv_mid, conv_out, time_weight):
    slot, n, strips = lax.axis_index("tm"), lax.axis_size("tm"), lax.axis_size("rows")
    hidden, chans, rows, cols = conv_mid.shape[2], x_start.shape[1], x_start.shape[2], x_start.shape[3]
    hops = (n - 1).bit_length()
    table = plan_table(STEPS)
    spots = [lax.dynamic_slice_in_dim(sched, slot + RETIRE * r, 2, 0) for r in range(ROUNDS)]
    steps = jnp.stack(spots)
    logs = lookup(table, steps.reshape(-1)).reshape(ROUNDS, 2)
    coef = coefficients(logs[:, 0], logs[:, 1])
    features = time_features(steps[:, 0].astype(f32), hidden)
    embedding = jnp.dot(features, time_weight.astype(f32), precision=lax.Precision.HIGHEST)
    emb = jnp.broadcast_to(embedding[:, :, None], (ROUNDS, hidden, cols))
    frame = (rows, chans, cols)
    vmem, dma = pltpu.VMEM, pltpu.SemaphoreType.DMA
    result = pl.pallas_call(
        functools.partial(kernel, n, strips, hops),
        out_shape=jax.ShapeDtypeStruct((ROUNDS,) + frame, f32),
        in_specs=[pl.BlockSpec(memory_space=pltpu.SMEM)] + [
            pl.BlockSpec(memory_space=pltpu.VMEM if i == 3 else pltpu.HBM) for i in range(7)
        ],
        out_specs=pl.BlockSpec(memory_space=pltpu.VMEM),
        scratch_shapes=[
            vmem((chans, rows, cols), f32),
            vmem((chans, rows, cols), f32),
            vmem((chans, rows, cols), f32),
            vmem((9 * chans, hidden), bf16),
            vmem(conv_mid.shape, bf16),
            vmem((9 * chans, hidden), bf16),
            vmem(frame, f32),
            vmem(frame, f32),
            vmem((hidden, 9 * chans), bf16),
            vmem((hidden, 9 * hidden), bf16),
            vmem((rows + 2 * RIM, 3 * chans, cols), bf16),
            vmem((rows + 4, 3 * hidden, cols), bf16),
            vmem((rows + 2, 9 * chans, cols), f32),
            vmem(frame, f32),
            vmem(frame, f32),
            vmem(frame, f32),
            vmem((2,) + frame, f32),
            vmem((2,) + frame, f32),
            vmem(frame, f32),
            vmem((4,) + frame, bf16),
            vmem((4, 2, RIM, chans, cols), bf16),
            vmem(frame, bf16),
            vmem(frame, f32),
            vmem((4, hops) + frame, bf16),
            vmem((4, hops) + frame, bf16),
            vmem((2, 2) + frame, f32),
            vmem((2, 2) + frame, f32),
            dma((4, 2)),
            dma((4, 2)),
            dma((2,)),
            dma,
            dma,
            dma,
            dma,
            dma((4, hops, 2)),
            dma((4, hops, 2)),
            dma((2, 2)),
            dma((2, 2)),
            dma((3,)),
            dma,
            dma((6,)),
        ],
        compiler_params=pltpu.CompilerParams(has_side_effects=True, vmem_limit_bytes=56 * 2**20),
        cost_estimate=pl.CostEstimate(
            flops=8 * rows * cols * 9 * hidden * (hidden + 2 * chans),
            bytes_accessed=4 * 2**20,
            transcendentals=8 * rows * cols * hidden,
        ),
    )(coef, x_start, noise, fresh, emb, conv_in.transpose(0, 1, 3, 2).reshape(-1, hidden), conv_mid, conv_out.reshape(-1, hidden))
    return result.transpose(0, 2, 1, 3)[:, None, None]


def solution(mesh):
    placed = (
        P(None, None, "rows", None),
        P("tm", None, None, "rows", None),
        P(None, None, None, "rows", None),
        P(),
        P(),
        P(),
        P(),
        P(),
    )
    return jax.shard_map(
        shards,
        mesh=mesh,
        in_specs=placed,
        out_specs=P(None, "tm", None, None, "rows", None),
        check_vma=False,
    )
```

```python
import functools

import jax
import jax.numpy as jnp
import numpy as np
from jax import lax
from jax.experimental import pallas as pl
from jax.experimental.pallas import tpu as pltpu
from jax.sharding import PartitionSpec as P

STEPS = 1000
RETIRE = 5
ROUNDS = 2
RIM = 3

log_base = 9.210340371976184
MESH = pl.DeviceIdType.MESH
f32, bf16 = jnp.float32, jnp.bfloat16


def plan_table(total_steps):
    positions = np.arange(total_steps).astype(np.float64)
    betas = 0.0001 + (0.02 - 0.0001) * positions / (total_steps - 1)
    return jnp.asarray(np.cumsum(np.log(1.0 - betas)).astype(np.float32))


def lookup(table, position):
    hit = jnp.arange(table.shape[0])[None] == position[:, None]
    return jnp.sum(jnp.where(hit, table[None], 0.0), axis=1)


def coefficients(log_now, log_next):
    retained = jnp.exp(log_now - log_next)
    bar_now = jnp.exp(log_now)
    bar_next = jnp.exp(log_next)
    keep = 1.0 / jnp.sqrt(retained) - 1.0
    predict = -(1.0 - retained) / (jnp.sqrt(1.0 - bar_now) * jnp.sqrt(retained))
    spread = jnp.sqrt((1.0 - bar_next) / (1.0 - bar_now) * (1.0 - retained))
    return jnp.stack([keep, predict, spread], axis=1)


def time_features(now_value, width):
    half = width // 2
    freqs = jnp.exp(-log_base * jnp.arange(half).astype(f32) / half)
    angles = now_value[..., None] * freqs
    return jnp.concatenate([jnp.sin(angles), jnp.cos(angles)], axis=-1)


def silu(v):
    half = 0.5 * v
    return half + half * jnp.tanh(half)


def moved_right(v):
    lane = lax.broadcasted_iota(jnp.int32, v.shape, v.ndim - 1)
    return jnp.where(lane == 0, 0.0, pltpu.roll(v, 1, v.ndim - 1))


def moved_left(v):
    size = v.shape[-1]
    lane = lax.broadcasted_iota(jnp.int32, v.shape, v.ndim - 1)
    return jnp.where(lane == size - 1, 0.0, pltpu.roll(v, size - 1, v.ndim - 1))


def kernel(
    n, strips, hops,
    coef, x_far, z_far, fresh_far, emb, in_far, mid_far, out_far, out,
    x_raw, z_raw, fresh_raw, in_raw, mid_raw, w_out, x, z0, w_in, w_mid,
    st, first, middle, parts, state, exc, inc, nexc, ninc, base,
    sent_state, rim, arrived, z_arrived,
    snd, rcv, nsnd, nrcv,
    rim_ss, rim_rs, far_ss, mv_ss, mv_rs, z_ss, z_rs,
    scan_ss, scan_rs, nscan_ss, nscan_rs, base_ss, base_rs, load_s,
):
    me, strip = lax.axis_index("tm"), lax.axis_index("rows")
    rows, chans, cols = x.shape
    hidden = w_mid.shape[0]
    half = rows // 2
    stay = n - RETIRE
    pick = jnp.clip(me - stay, 0, fresh_far.shape[0] - 1)
    loads = [
        pltpu.make_async_copy(source, target, load_s.at[i])
        for i, (source, target) in enumerate((
            (x_far.at[0], x_raw), (in_far, in_raw), (mid_far, mid_raw),
            (out_far, w_out), (z_far.at[0, 0], z_raw), (fresh_far.at[pick, 0], fresh_raw),
        ))
    ]
    for load in loads:
        load.start()
    has_up, has_down = strip > 0, strip < strips - 1

    def remote(src, dst, ss, rs, slot, to_strip):
        return pltpu.make_async_remote_copy(
            src_ref=src, dst_ref=dst, send_sem=ss, recv_sem=rs,
            device_id=(jnp.clip(slot, 0, n - 1), jnp.clip(to_strip, 0, strips - 1)),
            device_id_type=MESH,
        )

    def rim_copy(k, side, slot, far):
        lo = rows - RIM if side == 0 else 0
        to = strip + 1 if side == 0 else strip - 1
        ss = far_ss.at[side] if far else rim_ss.at[k, side]
        return remote(sent_state.at[k, pl.ds(lo, RIM)], rim.at[k, side], ss, rim_rs.at[k, side], slot, to)

    def send_rim(k, slot, far, gate, start):
        for side, there in ((0, has_down), (1, has_up)):
            @pl.when(jnp.logical_and(gate, there))
            def _():
                copy = rim_copy(k, side, slot, far)
                copy.start() if start else copy.wait_send()

    def move_copy():
        return remote(sent_state.at[2], arrived, mv_ss, mv_rs, me - RETIRE, strip)

    def z_copy():
        return remote(z0, z_arrived, z_ss, z_rs, me - RETIRE, strip)

    def base_copy(to, lane):
        return remote(base, base, base_ss.at[lane], base_rs, to, strip)

    mate = RETIRE + 1 - 2 * (RETIRE % 2)
    low, high = min(RETIRE, mate), max(RETIRE, mate)
    base_moves = (
        (me == RETIRE, mate, 0),
        (jnp.logical_and(me <= high, me >= 2), me - 2, 1),
        (jnp.logical_and(me >= low, me + 2 < n), me + 2, 2),
    )

    def base_pass(gate):
        @pl.when(jnp.logical_and(gate, me != RETIRE))
        def _():
            base_copy(me, 0).wait_recv()

        for allowed, to, lane in base_moves:
            @pl.when(jnp.logical_and(gate, allowed))
            def _():
                base_copy(to, lane).start()

    def scan_copy(k, s, part):
        at = pl.ds(part * half, half)
        return remote(
            snd.at[k, s, at], rcv.at[k, s, at], scan_ss.at[k, s, part], scan_rs.at[k, s, part], me + 2**s, strip
        )

    def scan_send(k, s, part):
        if s >= hops:
            return

        @pl.when(me + 2**s < n)
        def _():
            at = pl.ds(part * half, half)
            if s > 0:
                snd[k, s, at] = inc[at].astype(bf16)
            scan_copy(k, s, part).start()

    def scan_take(k, s, part):
        if s >= hops:
            return

        @pl.when(me >= 2**s)
        def _():
            at = pl.ds(part * half, half)
            scan_copy(k, s, part).wait_recv()
            got = rcv[k, s, at].astype(f32)
            exc[at] += got
            if s + 1 < hops:
                inc[at] += got

    level, odd = me // 2, me % 2

    def nscan_copy(k, s):
        to = me + 1 - 2 * odd if s == 0 else me + 2
        return remote(nsnd.at[k, s], nrcv.at[k, s], nscan_ss.at[k, s], nscan_rs.at[k, s], to, strip)

    def spread_rows(v):
        v = v.astype(f32)
        return jnp.concatenate([moved_right(v), v, moved_left(v)], axis=-2).astype(bf16)

    def expand(source, at, count):
        for i in range(count):
            st[at + i] = spread_rows(source[i])

    def noise_start(k, z):
        nsnd[k, 0] = coef[k, 2] * z[...]
        nscan_copy(k, 0).start()

    def noise_pair(k):
        nscan_copy(k, 0).wait_recv()
        ninc[k] = nsnd[k, 0] + nrcv[k, 0]
        nexc[k] = nrcv[k, 0] * odd.astype(f32)

    def noise_pass(k, gate):
        @pl.when(jnp.logical_and(gate, level > 0))
        def _():
            nscan_copy(k, 1).wait_recv()
            nexc[k] += nrcv[k, 1]
            ninc[k] += nrcv[k, 1]

        @pl.when(jnp.logical_and(gate, me + 2 < n))
        def _():
            nsnd[k, 1] = ninc[k]
            nscan_copy(k, 1).start()

    def sweep(k, r, noise, hooks=()):
        keep, predict, spread = coef[r, 0], coef[r, 1], coef[r, 2]
        up_scale, down_scale = has_up.astype(f32), has_down.astype(f32)
        in_steps, mid_steps = (rows + 4) // 2, (rows + 2) // 2

        def in_step(i, scale=None):
            f = 2 * i
            both = jnp.concatenate(
                [st[pl.ds(f + t, 3)].reshape(9 * chans, cols) for t in range(2)], axis=1
            )
            h = jnp.dot(w_in[...], both, preferred_element_type=f32)
            for t in range(2):
                v = silu(h[:, t * cols : (t + 1) * cols] + emb[r])
                if scale is not None:
                    v = v * scale
                first[f + t] = spread_rows(v)

        def mid_step(i):
            f = 2 * i
            both = jnp.concatenate(
                [first[pl.ds(f + t, 3)].reshape(9 * hidden, cols) for t in range(2)], axis=1
            )
            middle[...] = jnp.dot(w_mid[...], both, preferred_element_type=f32)

        def out_step(i):
            g = silu(middle[...]).astype(bf16)
            p = jnp.dot(w_out[...], g, preferred_element_type=f32)
            parts[2 * i] = p[:, :cols] * jnp.where(i == 0, up_scale, 1.0)
            parts[2 * i + 1] = p[:, cols:] * jnp.where(i == mid_steps - 1, down_scale, 1.0)

        def finish(y):
            sums = [
                sum(parts[y + a, (3 * a + b) * chans : (3 * a + b + 1) * chans] for a in range(3))
                for b in range(3)
            ]
            predicted = moved_right(sums[0]) + sums[1] + moved_left(sums[2])
            c = keep * state[y] + predict * predicted
            if noise is not None:
                c = c + spread * noise[y]
            inc[y] = c
            exc[y] = jnp.zeros_like(c)
            snd[k, 0, y] = c.astype(bf16)

        def step(i, _):
            for t in range(2):
                finish(jnp.maximum(2 * i - 6 + t, 0))
            out_step(jnp.maximum(i - 1, 0))
            mid_step(i)
            in_step(i + 2, jnp.where(i + 2 == in_steps - 1, down_scale, 1.0))
            for at, hook in hooks:
                pl.when(i == at)(hook)
            pl.when(i == half // 2 + 2)(lambda: scan_send(k, 0, 0))
            return 0

        in_step(0, up_scale)
        in_step(1)
        lax.fori_loop(0, mid_steps, step, 0)
        out_step(mid_steps - 1)
        for y in range(rows - 4, rows):
            finish(y)
        scan_send(k, 0, 1)
        for s in range(hops):
            scan_take(k, s, 0)
            scan_send(k, s + 1, 0)
            scan_take(k, s, 1)
            scan_send(k, s + 1, 1)

    def take_rim(k):
        for side, there in ((0, has_up), (1, has_down)):
            @pl.when(there)
            def _():
                rim_copy(k, side, me, False).wait_recv()
                expand(rim.at[k, side], 0 if side == 0 else rows + RIM, RIM)

    yes = me >= 0
    early, late = 2, rows // 2 - 1

    loads[0].wait()
    x[...] = jnp.swapaxes(x_raw[...], 0, 1)
    sent_state[0] = x[...].astype(bf16)
    send_rim(0, me, False, yes, True)
    loads[4].wait()
    z0[...] = jnp.swapaxes(z_raw[...], 0, 1)

    @pl.when(me >= RETIRE)
    def _():
        z_copy().start()

    noise_start(0, z0)
    state[...] = x[...]

    @pl.when(jnp.logical_not(has_up))
    def _():
        st[pl.ds(0, RIM)] = jnp.zeros((RIM,) + st.shape[1:], bf16)

    @pl.when(jnp.logical_not(has_down))
    def _():
        st[pl.ds(rows + RIM, RIM)] = jnp.zeros((RIM,) + st.shape[1:], bf16)

    st[pl.ds(rows + 2 * RIM, 2)] = jnp.zeros((2,) + st.shape[1:], bf16)
    middle[...] = jnp.zeros(middle.shape, f32)
    parts[...] = jnp.zeros(parts.shape, f32)
    expand(x, RIM, rows)
    for i in (1, 2, 3, 5):
        loads[i].wait()
    taps = [(a, b) for a in range(3) for b in range(3)]
    w_in[...] = in_raw[...].astype(f32).T.astype(bf16)
    w_mid[...] = jnp.concatenate([mid_raw[a, b] for a, b in taps], axis=1)
    take_rim(0)
    def first_pairs():
        noise_pair(0)
        noise_pass(0, level == 0)

    sweep(0, 0, z0, ((early, first_pairs),))
    state[...] = x[...] + exc[...]
    sent_state[1] = state[...].astype(bf16)
    send_rim(1, me, False, yes, True)
    expand(state, RIM, rows)
    noise_pass(0, level == 1)

    @pl.when(me < stay)
    def _():
        z_copy().wait_recv()

    @pl.when(me >= stay)
    def _():
        z_arrived[...] = jnp.swapaxes(fresh_raw[...], 0, 1)

    noise_start(1, z_arrived)

    take_rim(1)
    def second_pairs():
        noise_pass(0, level == 2)
        noise_pair(1)
        noise_pass(1, level == 0)

    sweep(1, 0, None, ((early, second_pairs),))
    noise_pass(0, level >= 3)
    state[...] = x[...] + (nexc[0] + exc[...])
    out[0] = state[...]

    sent_state[2] = state[...].astype(bf16)

    @pl.when(me >= RETIRE)
    def _():
        move_copy().start()

    send_rim(2, me - RETIRE, True, me >= RETIRE, True)
    send_rim(2, me, False, me >= stay, True)

    @pl.when(me == RETIRE)
    def _():
        base[...] = state[...]

    base_pass(me == RETIRE)
    noise_pass(1, level == 1)

    @pl.when(me < stay)
    def _():
        move_copy().wait_recv()
        state[...] = arrived[...].astype(f32)

    expand(state, RIM, rows)
    take_rim(2)
    near = jnp.logical_or(me == mate, me == RETIRE - 2)
    next_near = me == mate - 2

    def base_far():
        base_pass(next_near)
        noise_pass(1, level == 2)

    sweep(2, 1, z_arrived, ((early, lambda: base_pass(near)), (late, base_far)))

    base_pass(jnp.logical_not(jnp.logical_or(me == RETIRE, jnp.logical_or(near, next_near))))
    state[...] = base[...] + exc[...]
    sent_state[3] = state[...].astype(bf16)
    send_rim(3, me, False, yes, True)
    expand(state, RIM, rows)
    take_rim(3)
    sweep(3, 1, None)
    noise_pass(1, level >= 3)
    out[1] = base[...] + (nexc[1] + exc[...])

    for k, gate in ((0, yes), (1, yes), (2, me >= stay), (3, yes)):
        send_rim(k, me, False, gate, False)
    send_rim(2, me - RETIRE, True, me >= RETIRE, False)

    @pl.when(me >= RETIRE)
    def _():
        z_copy().wait_send()
        move_copy().wait_send()

    for allowed, to, lane in base_moves:
        @pl.when(allowed)
        def _():
            base_copy(to, lane).wait_send()

    for k in range(2):
        nscan_copy(k, 0).wait_send()

        @pl.when(me + 2 < n)
        def _():
            nscan_copy(k, 1).wait_send()

    for s in range(hops):
        @pl.when(me + 2**s < n)
        def _():
            for k in range(4):
                scan_copy(k, s, 0).wait_send()
                scan_copy(k, s, 1).wait_send()


def shards(x_start, noise, fresh, sched, conv_in, conv_mid, conv_out, time_weight):
    slot, n, strips = lax.axis_index("tm"), lax.axis_size("tm"), lax.axis_size("rows")
    hidden, chans, rows, cols = conv_mid.shape[2], x_start.shape[1], x_start.shape[2], x_start.shape[3]
    hops = (n - 1).bit_length()
    table = plan_table(STEPS)
    spots = [lax.dynamic_slice_in_dim(sched, slot + RETIRE * r, 2, 0) for r in range(ROUNDS)]
    steps = jnp.stack(spots)
    logs = lookup(table, steps.reshape(-1)).reshape(ROUNDS, 2)
    coef = coefficients(logs[:, 0], logs[:, 1])
    features = time_features(steps[:, 0].astype(f32), hidden)
    embedding = jnp.dot(features, time_weight.astype(f32), precision=lax.Precision.HIGHEST)
    emb = jnp.broadcast_to(embedding[:, :, None], (ROUNDS, hidden, cols))
    frame = (rows, chans, cols)
    vmem, dma = pltpu.VMEM, pltpu.SemaphoreType.DMA
    result = pl.pallas_call(
        functools.partial(kernel, n, strips, hops),
        out_shape=jax.ShapeDtypeStruct((ROUNDS,) + frame, f32),
        in_specs=[pl.BlockSpec(memory_space=pltpu.SMEM)] + [
            pl.BlockSpec(memory_space=pltpu.VMEM if i == 3 else pltpu.HBM) for i in range(7)
        ],
        out_specs=pl.BlockSpec(memory_space=pltpu.VMEM),
        scratch_shapes=[
            vmem((chans, rows, cols), f32),
            vmem((chans, rows, cols), f32),
            vmem((chans, rows, cols), f32),
            vmem((9 * chans, hidden), bf16),
            vmem(conv_mid.shape, bf16),
            vmem((9 * chans, hidden), bf16),
            vmem(frame, f32),
            vmem(frame, f32),
            vmem((hidden, 9 * chans), bf16),
            vmem((hidden, 9 * hidden), bf16),
            vmem((rows + 2 * RIM + 2, 3 * chans, cols), bf16),
            vmem((rows + 6, 3 * hidden, cols), bf16),
            vmem((hidden, 2 * cols), f32),
            vmem((rows + 2, 9 * chans, cols), f32),
            vmem(frame, f32),
            vmem(frame, f32),
            vmem(frame, f32),
            vmem((2,) + frame, f32),
            vmem((2,) + frame, f32),
            vmem(frame, f32),
            vmem((4,) + frame, bf16),
            vmem((4, 2, RIM, chans, cols), bf16),
            vmem(frame, bf16),
            vmem(frame, f32),
            vmem((4, hops) + frame, bf16),
            vmem((4, hops) + frame, bf16),
            vmem((2, 2) + frame, f32),
            vmem((2, 2) + frame, f32),
            dma((4, 2)),
            dma((4, 2)),
            dma((2,)),
            dma,
            dma,
            dma,
            dma,
            dma((4, hops, 2)),
            dma((4, hops, 2)),
            dma((2, 2)),
            dma((2, 2)),
            dma((3,)),
            dma,
            dma((6,)),
        ],
        compiler_params=pltpu.CompilerParams(has_side_effects=True, vmem_limit_bytes=56 * 2**20),
        cost_estimate=pl.CostEstimate(
            flops=8 * rows * cols * 9 * hidden * (hidden + 2 * chans),
            bytes_accessed=4 * 2**20,
            transcendentals=8 * rows * cols * hidden,
        ),
    )(coef, x_start, noise, fresh, emb, conv_in.transpose(0, 1, 3, 2).reshape(-1, hidden), conv_mid, conv_out.reshape(-1, hidden))
    return result.transpose(0, 2, 1, 3)[:, None, None]


def solution(mesh):
    placed = (
        P(None, None, "rows", None),
        P("tm", None, None, "rows", None),
        P(None, None, None, "rows", None),
        P(),
        P(),
        P(),
        P(),
        P(),
    )
    return jax.shard_map(
        shards,
        mesh=mesh,
        in_specs=placed,
        out_specs=P(None, "tm", None, None, "rows", None),
        check_vma=False,
    )
```

```python
import functools

import jax
import jax.numpy as jnp
import numpy as np
from jax import lax
from jax.experimental import pallas as pl
from jax.experimental.pallas import tpu as pltpu
from jax.sharding import PartitionSpec as P

STEPS = 1000
RETIRE = 5
ROUNDS = 2
RIM = 3

log_base = 9.210340371976184
MESH = pl.DeviceIdType.MESH
f32, bf16 = jnp.float32, jnp.bfloat16


def plan_table(total_steps):
    positions = np.arange(total_steps).astype(np.float64)
    betas = 0.0001 + (0.02 - 0.0001) * positions / (total_steps - 1)
    return jnp.asarray(np.cumsum(np.log(1.0 - betas)).astype(np.float32))


def lookup(table, position):
    hit = jnp.arange(table.shape[0])[None] == position[:, None]
    return jnp.sum(jnp.where(hit, table[None], 0.0), axis=1)


def coefficients(log_now, log_next):
    retained = jnp.exp(log_now - log_next)
    bar_now = jnp.exp(log_now)
    bar_next = jnp.exp(log_next)
    keep = 1.0 / jnp.sqrt(retained) - 1.0
    predict = -(1.0 - retained) / (jnp.sqrt(1.0 - bar_now) * jnp.sqrt(retained))
    spread = jnp.sqrt((1.0 - bar_next) / (1.0 - bar_now) * (1.0 - retained))
    return jnp.stack([keep, predict, spread], axis=1)


def time_features(now_value, width):
    half = width // 2
    freqs = jnp.exp(-log_base * jnp.arange(half).astype(f32) / half)
    angles = now_value[..., None] * freqs
    return jnp.concatenate([jnp.sin(angles), jnp.cos(angles)], axis=-1)


def silu(v):
    half = 0.5 * v
    return half + half * jnp.tanh(half)


def moved_right(v):
    lane = lax.broadcasted_iota(jnp.int32, v.shape, v.ndim - 1)
    return jnp.where(lane == 0, jnp.zeros_like(v), pltpu.roll(v, 1, v.ndim - 1))


def moved_left(v):
    size = v.shape[-1]
    lane = lax.broadcasted_iota(jnp.int32, v.shape, v.ndim - 1)
    return jnp.where(lane == size - 1, jnp.zeros_like(v), pltpu.roll(v, size - 1, v.ndim - 1))


def kernel(
    n, strips, hops,
    coef, x_far, z_far, fresh_far, emb, in_far, mid_far, out_far, out,
    x_raw, z_raw, fresh_raw, in_raw, mid_raw, w_out, x, z0, w_in, w_mid,
    st, first, middle, parts, state, exc, inc, nexc, ninc, base,
    sent_state, rim, arrived, z_arrived,
    snd, rcv, nsnd, nrcv,
    rim_ss, rim_rs, far_ss, mv_ss, mv_rs, z_ss, z_rs,
    scan_ss, scan_rs, nscan_ss, nscan_rs, base_ss, base_rs, load_s,
):
    me, strip = lax.axis_index("tm"), lax.axis_index("rows")
    rows, chans, cols = x.shape
    hidden = w_mid.shape[0]
    half = rows // 2
    stay = n - RETIRE
    pick = jnp.clip(me - stay, 0, fresh_far.shape[0] - 1)
    loads = [
        pltpu.make_async_copy(source, target, load_s.at[i])
        for i, (source, target) in enumerate((
            (x_far.at[0], x_raw), (in_far, in_raw), (mid_far, mid_raw),
            (out_far, w_out), (z_far.at[0, 0], z_raw), (fresh_far.at[pick, 0], fresh_raw),
        ))
    ]
    for load in loads:
        load.start()
    has_up, has_down = strip > 0, strip < strips - 1

    def remote(src, dst, ss, rs, slot, to_strip):
        return pltpu.make_async_remote_copy(
            src_ref=src, dst_ref=dst, send_sem=ss, recv_sem=rs,
            device_id=(jnp.clip(slot, 0, n - 1), jnp.clip(to_strip, 0, strips - 1)),
            device_id_type=MESH,
        )

    def rim_copy(k, side, slot, far):
        lo = rows - RIM if side == 0 else 0
        to = strip + 1 if side == 0 else strip - 1
        ss = far_ss.at[side] if far else rim_ss.at[k, side]
        return remote(sent_state.at[k, pl.ds(lo, RIM)], rim.at[k, side], ss, rim_rs.at[k, side], slot, to)

    def send_rim(k, slot, far, gate, start):
        for side, there in ((0, has_down), (1, has_up)):
            @pl.when(jnp.logical_and(gate, there))
            def _():
                copy = rim_copy(k, side, slot, far)
                copy.start() if start else copy.wait_send()

    def move_copy():
        return remote(sent_state.at[2], arrived, mv_ss, mv_rs, me - RETIRE, strip)

    def z_copy():
        return remote(z0, z_arrived, z_ss, z_rs, me - RETIRE, strip)

    def base_copy(to, lane):
        return remote(base, base, base_ss.at[lane], base_rs, to, strip)

    mate = RETIRE + 1 - 2 * (RETIRE % 2)
    low, high = min(RETIRE, mate), max(RETIRE, mate)
    base_moves = (
        (me == RETIRE, mate, 0),
        (jnp.logical_and(me <= high, me >= 2), me - 2, 1),
        (jnp.logical_and(me >= low, me + 2 < n), me + 2, 2),
    )

    def base_pass(gate):
        @pl.when(jnp.logical_and(gate, me != RETIRE))
        def _():
            base_copy(me, 0).wait_recv()

        for allowed, to, lane in base_moves:
            @pl.when(jnp.logical_and(gate, allowed))
            def _():
                base_copy(to, lane).start()

    def scan_copy(k, s, part):
        at = pl.ds(part * half, half)
        return remote(
            snd.at[k, s, at], rcv.at[k, s, at], scan_ss.at[k, s, part], scan_rs.at[k, s, part], me + 2**s, strip
        )

    def scan_send(k, s, part):
        if s >= hops:
            return

        @pl.when(me + 2**s < n)
        def _():
            at = pl.ds(part * half, half)
            if s > 0:
                snd[k, s, at] = inc[at].astype(bf16)
            scan_copy(k, s, part).start()

    def scan_take(k, s, part):
        if s >= hops:
            return

        @pl.when(me >= 2**s)
        def _():
            at = pl.ds(part * half, half)
            scan_copy(k, s, part).wait_recv()
            got = rcv[k, s, at].astype(f32)
            exc[at] += got
            if s + 1 < hops:
                inc[at] += got

    level, odd = me // 2, me % 2

    def nscan_copy(k, s):
        to = me + 1 - 2 * odd if s == 0 else me + 2
        return remote(nsnd.at[k, s], nrcv.at[k, s], nscan_ss.at[k, s], nscan_rs.at[k, s], to, strip)

    def spread_rows(v):
        v = v.astype(bf16)
        return jnp.concatenate([moved_right(v), v, moved_left(v)], axis=-2)

    def expand(source, at, count):
        for i in range(count):
            st[at + i] = spread_rows(source[i])

    def noise_start(k, z):
        nsnd[k, 0] = coef[k, 2] * z[...]
        nscan_copy(k, 0).start()

    def noise_pair(k):
        nscan_copy(k, 0).wait_recv()
        ninc[k] = nsnd[k, 0] + nrcv[k, 0]
        nexc[k] = nrcv[k, 0] * odd.astype(f32)

    def noise_pass(k, gate):
        @pl.when(jnp.logical_and(gate, level > 0))
        def _():
            nscan_copy(k, 1).wait_recv()
            nexc[k] += nrcv[k, 1]
            ninc[k] += nrcv[k, 1]

        @pl.when(jnp.logical_and(gate, me + 2 < n))
        def _():
            nsnd[k, 1] = ninc[k]
            nscan_copy(k, 1).start()

    def sweep(k, r, noise, hooks=()):
        keep, predict, spread = coef[r, 0], coef[r, 1], coef[r, 2]
        up_scale, down_scale = has_up.astype(f32), has_down.astype(f32)
        in_steps, mid_steps = (rows + 4) // 2, (rows + 2) // 2

        def in_step(i, scale=None):
            f = 2 * i
            both = jnp.concatenate(
                [st[pl.ds(f + t, 3)].reshape(9 * chans, cols) for t in range(2)], axis=1
            )
            h = jnp.dot(w_in[...], both, preferred_element_type=f32)
            for t in range(2):
                v = silu(h[:, t * cols : (t + 1) * cols] + emb[r])
                if scale is not None:
                    v = v * scale
                first[f + t] = spread_rows(v)

        def mid_step(i):
            f = 2 * i
            both = jnp.concatenate(
                [first[pl.ds(f + t, 3)].reshape(9 * hidden, cols) for t in range(2)], axis=1
            )
            middle[...] = jnp.dot(w_mid[...], both, preferred_element_type=f32)

        def out_step(i):
            g = silu(middle[...]).astype(bf16)
            p = jnp.dot(w_out[...], g, preferred_element_type=f32)
            parts[2 * i] = p[:, :cols] * jnp.where(i == 0, up_scale, 1.0)
            parts[2 * i + 1] = p[:, cols:] * jnp.where(i == mid_steps - 1, down_scale, 1.0)

        def finish(y):
            sums = [
                sum(parts[y + a, (3 * a + b) * chans : (3 * a + b + 1) * chans] for a in range(3))
                for b in range(3)
            ]
            predicted = moved_right(sums[0]) + sums[1] + moved_left(sums[2])
            c = keep * state[y] + predict * predicted
            if noise is not None:
                c = c + spread * noise[y]
            inc[y] = c
            exc[y] = jnp.zeros_like(c)
            snd[k, 0, y] = c.astype(bf16)

        def step(i, _):
            for t in range(2):
                finish(jnp.maximum(2 * i - 6 + t, 0))
            out_step(jnp.maximum(i - 1, 0))
            mid_step(i)
            in_step(i + 2, jnp.where(i + 2 == in_steps - 1, down_scale, 1.0))
            for at, hook in hooks:
                pl.when(i == at)(hook)
            pl.when(i == half // 2 + 2)(lambda: scan_send(k, 0, 0))
            return 0

        in_step(0, up_scale)
        in_step(1)
        lax.fori_loop(0, mid_steps, step, 0)
        scan_take(k, 0, 0)
        scan_send(k, 1, 0)
        out_step(mid_steps - 1)
        for y in range(rows - 4, rows):
            finish(y)
        scan_send(k, 0, 1)
        for s in range(hops):
            if s > 0:
                scan_take(k, s, 0)
                scan_send(k, s + 1, 0)
            scan_take(k, s, 1)
            scan_send(k, s + 1, 1)

    def take_rim(k):
        for side, there in ((0, has_up), (1, has_down)):
            @pl.when(there)
            def _():
                rim_copy(k, side, me, False).wait_recv()
                expand(rim.at[k, side], 0 if side == 0 else rows + RIM, RIM)

    yes = me >= 0
    early, late = 2, rows // 2 - 1

    loads[0].wait()
    x[...] = jnp.swapaxes(x_raw[...], 0, 1)
    sent_state[0] = x[...].astype(bf16)
    send_rim(0, me, False, yes, True)
    loads[4].wait()
    z0[...] = jnp.swapaxes(z_raw[...], 0, 1)

    @pl.when(me >= RETIRE)
    def _():
        z_copy().start()

    noise_start(0, z0)
    state[...] = x[...]

    @pl.when(jnp.logical_not(has_up))
    def _():
        st[pl.ds(0, RIM)] = jnp.zeros((RIM,) + st.shape[1:], bf16)

    @pl.when(jnp.logical_not(has_down))
    def _():
        st[pl.ds(rows + RIM, RIM)] = jnp.zeros((RIM,) + st.shape[1:], bf16)

    st[pl.ds(rows + 2 * RIM, 2)] = jnp.zeros((2,) + st.shape[1:], bf16)
    middle[...] = jnp.zeros(middle.shape, f32)
    parts[...] = jnp.zeros(parts.shape, f32)
    expand(x, RIM, rows)
    for i in (1, 2, 3, 5):
        loads[i].wait()
    taps = [(a, b) for a in range(3) for b in range(3)]
    w_in[...] = in_raw[...].astype(f32).T.astype(bf16)
    w_mid[...] = jnp.concatenate([mid_raw[a, b] for a, b in taps], axis=1)
    take_rim(0)
    def first_pairs():
        noise_pair(0)
        noise_pass(0, level == 0)

    sweep(0, 0, z0, ((early, first_pairs),))
    state[...] = x[...] + exc[...]
    sent_state[1] = state[...].astype(bf16)
    send_rim(1, me, False, yes, True)
    expand(state, RIM, rows)
    noise_pass(0, level == 1)

    @pl.when(me < stay)
    def _():
        z_copy().wait_recv()

    @pl.when(me >= stay)
    def _():
        z_arrived[...] = jnp.swapaxes(fresh_raw[...], 0, 1)

    noise_start(1, z_arrived)

    take_rim(1)
    def second_pairs():
        noise_pass(0, level == 2)
        noise_pair(1)
        noise_pass(1, level == 0)

    sweep(1, 0, None, ((early, second_pairs),))
    noise_pass(0, level >= 3)
    state[...] = x[...] + (nexc[0] + exc[...])
    out[0] = state[...]

    sent_state[2] = state[...].astype(bf16)

    @pl.when(me >= RETIRE)
    def _():
        move_copy().start()

    send_rim(2, me - RETIRE, True, me >= RETIRE, True)
    send_rim(2, me, False, me >= stay, True)

    @pl.when(me == RETIRE)
    def _():
        base[...] = state[...]

    base_pass(me == RETIRE)
    noise_pass(1, level == 1)

    @pl.when(me < stay)
    def _():
        move_copy().wait_recv()
        state[...] = arrived[...].astype(f32)

    expand(state, RIM, rows)
    take_rim(2)
    near = jnp.logical_or(me == mate, me == RETIRE - 2)
    next_near = me == mate - 2

    def base_far():
        base_pass(next_near)
        noise_pass(1, level == 2)

    sweep(2, 1, z_arrived, ((early, lambda: base_pass(near)), (late, base_far)))

    base_pass(jnp.logical_not(jnp.logical_or(me == RETIRE, jnp.logical_or(near, next_near))))
    state[...] = base[...] + exc[...]
    sent_state[3] = state[...].astype(bf16)
    send_rim(3, me, False, yes, True)
    expand(state, RIM, rows)
    take_rim(3)
    sweep(3, 1, None)
    noise_pass(1, level >= 3)
    out[1] = base[...] + (nexc[1] + exc[...])

    for k, gate in ((0, yes), (1, yes), (2, me >= stay), (3, yes)):
        send_rim(k, me, False, gate, False)
    send_rim(2, me - RETIRE, True, me >= RETIRE, False)

    @pl.when(me >= RETIRE)
    def _():
        z_copy().wait_send()
        move_copy().wait_send()

    for allowed, to, lane in base_moves:
        @pl.when(allowed)
        def _():
            base_copy(to, lane).wait_send()

    for k in range(2):
        nscan_copy(k, 0).wait_send()

        @pl.when(me + 2 < n)
        def _():
            nscan_copy(k, 1).wait_send()

    for s in range(hops):
        @pl.when(me + 2**s < n)
        def _():
            for k in range(4):
                scan_copy(k, s, 0).wait_send()
                scan_copy(k, s, 1).wait_send()


def shards(x_start, noise, fresh, sched, conv_in, conv_mid, conv_out, time_weight):
    slot, n, strips = lax.axis_index("tm"), lax.axis_size("tm"), lax.axis_size("rows")
    hidden, chans, rows, cols = conv_mid.shape[2], x_start.shape[1], x_start.shape[2], x_start.shape[3]
    hops = (n - 1).bit_length()
    table = plan_table(STEPS)
    spots = [lax.dynamic_slice_in_dim(sched, slot + RETIRE * r, 2, 0) for r in range(ROUNDS)]
    steps = jnp.stack(spots)
    logs = lookup(table, steps.reshape(-1)).reshape(ROUNDS, 2)
    coef = coefficients(logs[:, 0], logs[:, 1])
    features = time_features(steps[:, 0].astype(f32), hidden)
    embedding = jnp.dot(features, time_weight.astype(f32), precision=lax.Precision.HIGHEST)
    emb = jnp.broadcast_to(embedding[:, :, None], (ROUNDS, hidden, cols))
    frame = (rows, chans, cols)
    vmem, dma = pltpu.VMEM, pltpu.SemaphoreType.DMA
    result = pl.pallas_call(
        functools.partial(kernel, n, strips, hops),
        out_shape=jax.ShapeDtypeStruct((ROUNDS,) + frame, f32),
        in_specs=[pl.BlockSpec(memory_space=pltpu.SMEM)] + [
            pl.BlockSpec(memory_space=pltpu.VMEM if i == 3 else pltpu.HBM) for i in range(7)
        ],
        out_specs=pl.BlockSpec(memory_space=pltpu.VMEM),
        scratch_shapes=[
            vmem((chans, rows, cols), f32),
            vmem((chans, rows, cols), f32),
            vmem((chans, rows, cols), f32),
            vmem((9 * chans, hidden), bf16),
            vmem(conv_mid.shape, bf16),
            vmem((9 * chans, hidden), bf16),
            vmem(frame, f32),
            vmem(frame, f32),
            vmem((hidden, 9 * chans), bf16),
            vmem((hidden, 9 * hidden), bf16),
            vmem((rows + 2 * RIM + 2, 3 * chans, cols), bf16),
            vmem((rows + 6, 3 * hidden, cols), bf16),
            vmem((hidden, 2 * cols), f32),
            vmem((rows + 2, 9 * chans, cols), f32),
            vmem(frame, f32),
            vmem(frame, f32),
            vmem(frame, f32),
            vmem((2,) + frame, f32),
            vmem((2,) + frame, f32),
            vmem(frame, f32),
            vmem((4,) + frame, bf16),
            vmem((4, 2, RIM, chans, cols), bf16),
            vmem(frame, bf16),
            vmem(frame, f32),
            vmem((4, hops) + frame, bf16),
            vmem((4, hops) + frame, bf16),
            vmem((2, 2) + frame, f32),
            vmem((2, 2) + frame, f32),
            dma((4, 2)),
            dma((4, 2)),
            dma((2,)),
            dma,
            dma,
            dma,
            dma,
            dma((4, hops, 2)),
            dma((4, hops, 2)),
            dma((2, 2)),
            dma((2, 2)),
            dma((3,)),
            dma,
            dma((6,)),
        ],
        compiler_params=pltpu.CompilerParams(has_side_effects=True, vmem_limit_bytes=56 * 2**20),
        cost_estimate=pl.CostEstimate(
            flops=8 * rows * cols * 9 * hidden * (hidden + 2 * chans),
            bytes_accessed=4 * 2**20,
            transcendentals=8 * rows * cols * hidden,
        ),
    )(coef, x_start, noise, fresh, emb, conv_in.transpose(0, 1, 3, 2).reshape(-1, hidden), conv_mid, conv_out.reshape(-1, hidden))
    return result.transpose(0, 2, 1, 3)[:, None, None]


def solution(mesh):
    placed = (
        P(None, None, "rows", None),
        P("tm", None, None, "rows", None),
        P(None, None, None, "rows", None),
        P(),
        P(),
        P(),
        P(),
        P(),
    )
    return jax.shard_map(
        shards,
        mesh=mesh,
        in_specs=placed,
        out_specs=P(None, "tm", None, None, "rows", None),
        check_vma=False,
    )
```

```python
import functools

import jax
import jax.numpy as jnp
import numpy as np
from jax import lax
from jax.experimental import pallas as pl
from jax.experimental.pallas import tpu as pltpu
from jax.sharding import PartitionSpec as P

STEPS = 1000
RETIRE = 5
ROUNDS = 2
RIM = 3

log_base = 9.210340371976184
MESH = pl.DeviceIdType.MESH
f32, bf16 = jnp.float32, jnp.bfloat16


def plan_table(total_steps):
    positions = np.arange(total_steps).astype(np.float64)
    betas = 0.0001 + (0.02 - 0.0001) * positions / (total_steps - 1)
    return jnp.asarray(np.cumsum(np.log(1.0 - betas)).astype(np.float32))


def lookup(table, position):
    hit = jnp.arange(table.shape[0])[None] == position[:, None]
    return jnp.sum(jnp.where(hit, table[None], 0.0), axis=1)


def coefficients(log_now, log_next):
    retained = jnp.exp(log_now - log_next)
    bar_now = jnp.exp(log_now)
    bar_next = jnp.exp(log_next)
    keep = 1.0 / jnp.sqrt(retained) - 1.0
    predict = -(1.0 - retained) / (jnp.sqrt(1.0 - bar_now) * jnp.sqrt(retained))
    spread = jnp.sqrt((1.0 - bar_next) / (1.0 - bar_now) * (1.0 - retained))
    return jnp.stack([keep, predict, spread], axis=1)


def time_features(now_value, width):
    half = width // 2
    freqs = jnp.exp(-log_base * jnp.arange(half).astype(f32) / half)
    angles = now_value[..., None] * freqs
    return jnp.concatenate([jnp.sin(angles), jnp.cos(angles)], axis=-1)


def silu(v):
    half = 0.5 * v
    return half + half * jnp.tanh(half)


def moved_right(v):
    lane = lax.broadcasted_iota(jnp.int32, v.shape, v.ndim - 1)
    return jnp.where(lane == 0, 0.0, pltpu.roll(v, 1, v.ndim - 1))


def moved_left(v):
    size = v.shape[-1]
    lane = lax.broadcasted_iota(jnp.int32, v.shape, v.ndim - 1)
    return jnp.where(lane == size - 1, 0.0, pltpu.roll(v, size - 1, v.ndim - 1))


def kernel(
    n, strips, hops,
    coef, x_far, z_far, fresh_far, emb, in_far, mid_far, out_far, out,
    x_raw, z_raw, fresh_raw, in_raw, mid_raw, w_out, x, z0, w_in, w_mid,
    st, first, middle, parts, state, exc, inc, nexc, ninc, base,
    sent_state, rim, arrived, z_arrived,
    snd, rcv, nsnd, nrcv,
    rim_ss, rim_rs, far_ss, mv_ss, mv_rs, z_ss, z_rs,
    scan_ss, scan_rs, nscan_ss, nscan_rs, base_ss, base_rs, load_s,
):
    me, strip = lax.axis_index("tm"), lax.axis_index("rows")
    rows, chans, cols = x.shape
    hidden = w_mid.shape[0]
    half = rows // 2
    stay = n - RETIRE
    pick = jnp.clip(me - stay, 0, fresh_far.shape[0] - 1)
    loads = [
        pltpu.make_async_copy(source, target, load_s.at[i])
        for i, (source, target) in enumerate((
            (x_far.at[0], x_raw), (in_far, in_raw), (mid_far, mid_raw),
            (out_far, w_out), (z_far.at[0, 0], z_raw), (fresh_far.at[pick, 0], fresh_raw),
        ))
    ]
    for load in loads:
        load.start()
    has_up, has_down = strip > 0, strip < strips - 1

    def remote(src, dst, ss, rs, slot, to_strip):
        return pltpu.make_async_remote_copy(
            src_ref=src, dst_ref=dst, send_sem=ss, recv_sem=rs,
            device_id=(jnp.clip(slot, 0, n - 1), jnp.clip(to_strip, 0, strips - 1)),
            device_id_type=MESH,
        )

    def rim_copy(k, side, slot, far):
        lo = rows - RIM if side == 0 else 0
        to = strip + 1 if side == 0 else strip - 1
        ss = far_ss.at[side] if far else rim_ss.at[k, side]
        return remote(sent_state.at[k, pl.ds(lo, RIM)], rim.at[k, side], ss, rim_rs.at[k, side], slot, to)

    def send_rim(k, slot, far, gate, start):
        for side, there in ((0, has_down), (1, has_up)):
            @pl.when(jnp.logical_and(gate, there))
            def _():
                copy = rim_copy(k, side, slot, far)
                copy.start() if start else copy.wait_send()

    def move_copy():
        return remote(sent_state.at[2], arrived, mv_ss, mv_rs, me - RETIRE, strip)

    def z_copy():
        return remote(z0, z_arrived, z_ss, z_rs, me - RETIRE, strip)

    def base_copy(to, lane):
        return remote(base, base, base_ss.at[lane], base_rs, to, strip)

    mate = RETIRE + 1 - 2 * (RETIRE % 2)
    low, high = min(RETIRE, mate), max(RETIRE, mate)
    base_moves = (
        (me == RETIRE, mate, 0),
        (jnp.logical_and(me <= high, me >= 2), me - 2, 1),
        (jnp.logical_and(me >= low, me + 2 < n), me + 2, 2),
    )

    def base_pass(gate):
        @pl.when(jnp.logical_and(gate, me != RETIRE))
        def _():
            base_copy(me, 0).wait_recv()

        for allowed, to, lane in base_moves:
            @pl.when(jnp.logical_and(gate, allowed))
            def _():
                base_copy(to, lane).start()

    def scan_copy(k, s, part):
        at = pl.ds(part * half, half)
        return remote(
            snd.at[k, s, at], rcv.at[k, s, at], scan_ss.at[k, s, part], scan_rs.at[k, s, part], me + 2**s, strip
        )

    def scan_send(k, s, part):
        if s >= hops:
            return

        @pl.when(me + 2**s < n)
        def _():
            at = pl.ds(part * half, half)
            if s > 0:
                snd[k, s, at] = inc[at].astype(bf16)
            scan_copy(k, s, part).start()

    def scan_take(k, s, part):
        if s >= hops:
            return

        @pl.when(me >= 2**s)
        def _():
            at = pl.ds(part * half, half)
            scan_copy(k, s, part).wait_recv()
            got = rcv[k, s, at].astype(f32)
            exc[at] += got
            if s + 1 < hops:
                inc[at] += got

    level, odd = me // 2, me % 2

    def nscan_copy(k, s):
        to = me + 1 - 2 * odd if s == 0 else me + 2
        return remote(nsnd.at[k, s], nrcv.at[k, s], nscan_ss.at[k, s], nscan_rs.at[k, s], to, strip)

    def spread_rows(v):
        v = v.astype(f32)
        return jnp.concatenate([moved_right(v), v, moved_left(v)], axis=-2).astype(bf16)

    def expand(source, at, count):
        for i in range(count):
            st[at + i] = spread_rows(source[i])

    def noise_start(k, z):
        nsnd[k, 0] = coef[k, 2] * z[...]
        nscan_copy(k, 0).start()

    def noise_pair(k):
        nscan_copy(k, 0).wait_recv()
        ninc[k] = nsnd[k, 0] + nrcv[k, 0]
        nexc[k] = nrcv[k, 0] * odd.astype(f32)

    def noise_pass(k, gate):
        @pl.when(jnp.logical_and(gate, level > 0))
        def _():
            nscan_copy(k, 1).wait_recv()
            nexc[k] += nrcv[k, 1]
            ninc[k] += nrcv[k, 1]

        @pl.when(jnp.logical_and(gate, me + 2 < n))
        def _():
            nsnd[k, 1] = ninc[k]
            nscan_copy(k, 1).start()

    def sweep(k, r, noise, hooks=()):
        keep, predict, spread = coef[r, 0], coef[r, 1], coef[r, 2]
        up_scale, down_scale = has_up.astype(f32), has_down.astype(f32)
        in_steps, mid_steps = (rows + 4) // 2, (rows + 2) // 2

        def in_step(i, scale=None):
            f = 2 * i
            both = jnp.concatenate(
                [st[pl.ds(f + t, 3)].reshape(9 * chans, cols) for t in range(2)], axis=1
            )
            h = jnp.dot(w_in[...], both, preferred_element_type=f32)
            for t in range(2):
                v = silu(h[:, t * cols : (t + 1) * cols] + emb[r])
                if scale is not None:
                    v = v * scale
                first[f + t] = spread_rows(v)

        def mid_step(i):
            f = 2 * i
            both = jnp.concatenate(
                [first[pl.ds(f + t, 3)].reshape(9 * hidden, cols) for t in range(2)], axis=1
            )
            middle[...] = jnp.dot(w_mid[...], both, preferred_element_type=f32)

        def out_step(i):
            g = silu(middle[...]).astype(bf16)
            p = jnp.dot(w_out[...], g, preferred_element_type=f32)
            parts[2 * i] = p[:, :cols] * jnp.where(i == 0, up_scale, 1.0)
            parts[2 * i + 1] = p[:, cols:] * jnp.where(i == mid_steps - 1, down_scale, 1.0)

        def finish(y):
            sums = [
                sum(parts[y + a, (3 * a + b) * chans : (3 * a + b + 1) * chans] for a in range(3))
                for b in range(3)
            ]
            predicted = moved_right(sums[0]) + sums[1] + moved_left(sums[2])
            c = keep * state[y] + predict * predicted
            if noise is not None:
                c = c + spread * noise[y]
            inc[y] = c
            exc[y] = jnp.zeros_like(c)
            snd[k, 0, y] = c.astype(bf16)

        def step(i, _):
            for t in range(2):
                finish(jnp.maximum(2 * i - 6 + t, 0))
            out_step(jnp.maximum(i - 1, 0))
            mid_step(i)
            in_step(i + 2, jnp.where(i + 2 == in_steps - 1, down_scale, 1.0))
            for at, hook in hooks:
                pl.when(i == at)(hook)
            pl.when(i == half // 2 + 2)(lambda: scan_send(k, 0, 0))
            return 0

        in_step(0, up_scale)
        in_step(1)
        lax.fori_loop(0, mid_steps, step, 0)
        scan_take(k, 0, 0)
        scan_send(k, 1, 0)
        out_step(mid_steps - 1)
        for y in range(rows - 4, rows):
            finish(y)
        scan_send(k, 0, 1)
        for s in range(hops):
            if s > 0:
                scan_take(k, s, 0)
                scan_send(k, s + 1, 0)
            scan_take(k, s, 1)
            scan_send(k, s + 1, 1)

    def take_rim(k):
        for side, there in ((0, has_up), (1, has_down)):
            @pl.when(there)
            def _():
                rim_copy(k, side, me, False).wait_recv()
                expand(rim.at[k, side], 0 if side == 0 else rows + RIM, RIM)

    yes = me >= 0
    early, late = 2, rows // 2 - 1

    loads[0].wait()
    x[...] = jnp.swapaxes(x_raw[...], 0, 1)
    sent_state[0] = x[...].astype(bf16)
    send_rim(0, me, False, yes, True)
    loads[4].wait()
    z0[...] = jnp.swapaxes(z_raw[...], 0, 1)

    @pl.when(me >= RETIRE)
    def _():
        z_copy().start()

    noise_start(0, z0)
    state[...] = x[...]

    @pl.when(jnp.logical_not(has_up))
    def _():
        st[pl.ds(0, RIM)] = jnp.zeros((RIM,) + st.shape[1:], bf16)

    @pl.when(jnp.logical_not(has_down))
    def _():
        st[pl.ds(rows + RIM, RIM)] = jnp.zeros((RIM,) + st.shape[1:], bf16)

    st[pl.ds(rows + 2 * RIM, 2)] = jnp.zeros((2,) + st.shape[1:], bf16)
    middle[...] = jnp.zeros(middle.shape, f32)
    parts[...] = jnp.zeros(parts.shape, f32)
    expand(x, RIM, rows)
    for i in (1, 2, 3, 5):
        loads[i].wait()
    taps = [(a, b) for a in range(3) for b in range(3)]
    w_in[...] = in_raw[...].astype(f32).T.astype(bf16)
    w_mid[...] = jnp.concatenate([mid_raw[a, b] for a, b in taps], axis=1)
    take_rim(0)
    def first_pairs():
        noise_pair(0)
        noise_pass(0, level == 0)

    sweep(0, 0, z0, ((early, first_pairs),))
    state[...] = x[...] + exc[...]
    sent_state[1] = state[...].astype(bf16)
    send_rim(1, me, False, yes, True)
    expand(state, RIM, rows)
    noise_pass(0, level == 1)

    @pl.when(me < stay)
    def _():
        z_copy().wait_recv()

    @pl.when(me >= stay)
    def _():
        z_arrived[...] = jnp.swapaxes(fresh_raw[...], 0, 1)

    noise_start(1, z_arrived)

    take_rim(1)
    def second_pairs():
        noise_pass(0, level == 2)
        noise_pair(1)
        noise_pass(1, level == 0)

    sweep(1, 0, None, ((early, second_pairs),))
    noise_pass(0, level >= 3)
    state[...] = x[...] + (nexc[0] + exc[...])
    out[0] = state[...]

    sent_state[2] = state[...].astype(bf16)

    @pl.when(me >= RETIRE)
    def _():
        move_copy().start()

    send_rim(2, me - RETIRE, True, me >= RETIRE, True)
    send_rim(2, me, False, me >= stay, True)

    @pl.when(me == RETIRE)
    def _():
        base[...] = state[...]

    base_pass(me == RETIRE)
    noise_pass(1, level == 1)

    @pl.when(me < stay)
    def _():
        move_copy().wait_recv()
        state[...] = arrived[...].astype(f32)

    expand(state, RIM, rows)
    take_rim(2)
    near = jnp.logical_or(me == mate, me == RETIRE - 2)
    next_near = me == mate - 2

    def base_far():
        base_pass(next_near)
        noise_pass(1, level == 2)

    sweep(2, 1, z_arrived, ((early, lambda: base_pass(near)), (late, base_far)))

    base_pass(jnp.logical_not(jnp.logical_or(me == RETIRE, jnp.logical_or(near, next_near))))
    state[...] = base[...] + exc[...]
    sent_state[3] = state[...].astype(bf16)
    send_rim(3, me, False, yes, True)
    expand(state, RIM, rows)
    take_rim(3)
    sweep(3, 1, None)
    noise_pass(1, level >= 3)
    out[1] = base[...] + (nexc[1] + exc[...])

    for k, gate in ((0, yes), (1, yes), (2, me >= stay), (3, yes)):
        send_rim(k, me, False, gate, False)
    send_rim(2, me - RETIRE, True, me >= RETIRE, False)

    @pl.when(me >= RETIRE)
    def _():
        z_copy().wait_send()
        move_copy().wait_send()

    for allowed, to, lane in base_moves:
        @pl.when(allowed)
        def _():
            base_copy(to, lane).wait_send()

    for k in range(2):
        nscan_copy(k, 0).wait_send()

        @pl.when(me + 2 < n)
        def _():
            nscan_copy(k, 1).wait_send()

    for s in range(hops):
        @pl.when(me + 2**s < n)
        def _():
            for k in range(4):
                scan_copy(k, s, 0).wait_send()
                scan_copy(k, s, 1).wait_send()


def shards(x_start, noise, fresh, sched, conv_in, conv_mid, conv_out, time_weight):
    slot, n, strips = lax.axis_index("tm"), lax.axis_size("tm"), lax.axis_size("rows")
    hidden, chans, rows, cols = conv_mid.shape[2], x_start.shape[1], x_start.shape[2], x_start.shape[3]
    hops = (n - 1).bit_length()
    table = plan_table(STEPS)
    spots = [lax.dynamic_slice_in_dim(sched, slot + RETIRE * r, 2, 0) for r in range(ROUNDS)]
    steps = jnp.stack(spots)
    logs = lookup(table, steps.reshape(-1)).reshape(ROUNDS, 2)
    coef = coefficients(logs[:, 0], logs[:, 1])
    features = time_features(steps[:, 0].astype(f32), hidden)
    embedding = jnp.dot(features, time_weight.astype(f32), precision=lax.Precision.HIGHEST)
    emb = jnp.broadcast_to(embedding[:, :, None], (ROUNDS, hidden, cols))
    frame = (rows, chans, cols)
    vmem, dma = pltpu.VMEM, pltpu.SemaphoreType.DMA
    result = pl.pallas_call(
        functools.partial(kernel, n, strips, hops),
        out_shape=jax.ShapeDtypeStruct((ROUNDS,) + frame, f32),
        in_specs=[pl.BlockSpec(memory_space=pltpu.SMEM)] + [
            pl.BlockSpec(memory_space=pltpu.VMEM if i == 3 else pltpu.HBM) for i in range(7)
        ],
        out_specs=pl.BlockSpec(memory_space=pltpu.VMEM),
        scratch_shapes=[
            vmem((chans, rows, cols), f32),
            vmem((chans, rows, cols), f32),
            vmem((chans, rows, cols), f32),
            vmem((9 * chans, hidden), bf16),
            vmem(conv_mid.shape, bf16),
            vmem((9 * chans, hidden), bf16),
            vmem(frame, f32),
            vmem(frame, f32),
            vmem((hidden, 9 * chans), bf16),
            vmem((hidden, 9 * hidden), bf16),
            vmem((rows + 2 * RIM + 2, 3 * chans, cols), bf16),
            vmem((rows + 6, 3 * hidden, cols), bf16),
            vmem((hidden, 2 * cols), f32),
            vmem((rows + 2, 9 * chans, cols), f32),
            vmem(frame, f32),
            vmem(frame, f32),
            vmem(frame, f32),
            vmem((2,) + frame, f32),
            vmem((2,) + frame, f32),
            vmem(frame, f32),
            vmem((4,) + frame, bf16),
            vmem((4, 2, RIM, chans, cols), bf16),
            vmem(frame, bf16),
            vmem(frame, f32),
            vmem((4, hops) + frame, bf16),
            vmem((4, hops) + frame, bf16),
            vmem((2, 2) + frame, f32),
            vmem((2, 2) + frame, f32),
            dma((4, 2)),
            dma((4, 2)),
            dma((2,)),
            dma,
            dma,
            dma,
            dma,
            dma((4, hops, 2)),
            dma((4, hops, 2)),
            dma((2, 2)),
            dma((2, 2)),
            dma((3,)),
            dma,
            dma((6,)),
        ],
        compiler_params=pltpu.CompilerParams(has_side_effects=True, vmem_limit_bytes=56 * 2**20),
        cost_estimate=pl.CostEstimate(
            flops=8 * rows * cols * 9 * hidden * (hidden + 2 * chans),
            bytes_accessed=4 * 2**20,
            transcendentals=8 * rows * cols * hidden,
        ),
    )(coef, x_start, noise, fresh, emb, conv_in.transpose(0, 1, 3, 2).reshape(-1, hidden), conv_mid, conv_out.reshape(-1, hidden))
    return result.transpose(0, 2, 1, 3)[:, None, None]


def solution(mesh):
    placed = (
        P(None, None, "rows", None),
        P("tm", None, None, "rows", None),
        P(None, None, None, "rows", None),
        P(),
        P(),
        P(),
        P(),
        P(),
    )
    return jax.shard_map(
        shards,
        mesh=mesh,
        in_specs=placed,
        out_specs=P(None, "tm", None, None, "rows", None),
        check_vma=False,
    )
```
